32 devices in a mesh: row: 4 (over x, core), col: 4 (over z), tau: 2 (over y).
Axes of the slice: x: 2, y: 2, z: 4, core: 2. Of those that a mesh axis runs over, the one named last changes fastest.
Arguments:
- occ_states: bfloat16 [512, 512], P(('col', 'row')), may hold values from -0.25 to 0.25
- empty_states: bfloat16 [512, 4096], P(('col', 'row')), may hold values from -0.09375 to 0.09375
- mix_weights: float32 [4096, 16], replicated, may hold values from -4 to 4
- slice_of_block: int32 [128], replicated, may hold values from 0 to 23
- occ_energy: float32 [512], replicated, may hold values from -1.2 to -0.1
- pb_energy: float32 [384], replicated, may hold values from 0.1 to 2
- tau_points: float32 [6], P('tau'), may hold values from 0.05 to 2.5
- tau_weights: float32 [6], P('tau'), may hold values from 0.05 to 0.5
- trial: bfloat16 [512, 128], P(('col', 'row')), may hold values from -6 to 6
Outputs:
- trial_response: float32 [512, 128], P(('col', 'row'))
The draws below stay inside these ranges and needn't reach their ends.
All inputs are finite; a program needn't handle non-finite values.
Results may differ from the reference program's by a relative error of at most 0.0018.
Values may be sent and summed in bfloat16 or wider, within the bound.
No kernel may reach another device: no remote copies, remote signals or barrier semaphores. Data moves between devices by JAX's collectives and lax.ppermute only.
A program may use at most 64 MiB of HBM per device.

```python
import math
import jax
import jax.numpy as jnp
from jax import lax

NOCC = 512
NEMPTY = 4096
NPB = 384
PB_SLICE = 16
NV = 128
NPTS = 512
NTAU = 6
NSLICE = 24
NEBLK = 128


def set_ends(array, key, smallest, top_value):
    place = [jax.random.randint(jax.random.fold_in(key, axis), (), 0, length) for axis, length in enumerate(array.shape)]
    widest = array.shape.index(max(array.shape))
    beside = place[:widest] + [(place[widest] + 1) % array.shape[widest]] + place[widest + 1:]
    return array.at[tuple(place)].set(smallest).at[tuple(beside)].set(top_value)


def block_levels(rng, extent, split, low, largest):
    gain, own = 1.0, jax.random.fold_in(rng, 6)
    for dim, parts in split:
        steps = jnp.exp(jax.random.uniform(jax.random.fold_in(own, dim), (parts,), jnp.float32, low / len(split), largest / len(split)))
        gain = gain * jnp.repeat(steps, extent[dim] // parts).reshape([-1 if axis == dim else 1 for axis in range(len(extent))])
    return gain


def gaussian(stream_key, extent, deviation, limit, cuts=(), kind=jnp.bfloat16):
    array = jax.random.normal(stream_key, extent, jnp.float32) * deviation
    if len(cuts) > 0:
        array = block_levels(stream_key, extent, cuts, -0.22, 0.18) * array
    return jnp.clip(array, min=-limit, max=limit).astype(kind)


def setup_inputs(seed: int = 0) -> dict:
    seeds = jax.random.split(jax.random.key(seed), 10)
    occ_states = gaussian(seeds[0], (NPTS, NOCC), NOCC ** -0.5, 0.25, ((0, 16),))
    empty_states = gaussian(seeds[1], (NPTS, NEMPTY), NEMPTY ** -0.5, 0.09375, ((0, 16),))
    mix_weights = gaussian(seeds[2], (NEMPTY, PB_SLICE), 1.0, 4.0, (), jnp.float32)
    slice_of_block = set_ends(jax.random.randint(seeds[3], (NEBLK,), 0, NSLICE), jax.random.fold_in(seeds[3], 1), 0, NSLICE - 1).astype(jnp.int32)
    occ_energy = jnp.clip(jax.random.uniform(seeds[4], (NOCC,), jnp.float32, -1.2, -0.1), -1.2, -0.1)
    pb_energy = jnp.clip(jnp.exp(jax.random.uniform(seeds[5], (NPB,), jnp.float32, math.log(0.1), math.log(2.0))), 0.1, 2.0)
    tau_points = jnp.clip(jnp.exp(math.log(2.5) - 3.912023 * jax.random.uniform(seeds[6], (NTAU,), jnp.float32) ** block_levels(seeds[6], (NTAU,), ((0, 2),), -0.2, 0.2)), 0.05, 2.5)
    tau_weights = jnp.clip(jnp.exp(math.log(0.5) - 2.3025851 * jax.random.uniform(seeds[7], (NTAU,), jnp.float32) ** block_levels(seeds[7], (NTAU,), ((0, 2),), -0.2, 0.2)), 0.05, 0.5)
    trial = gaussian(seeds[8], (NPTS, NV), 1.0, 6.0, ((0, 16),))
    return {"occ_states": occ_states, "empty_states": empty_states, "mix_weights": mix_weights, "slice_of_block": slice_of_block, "occ_energy": occ_energy, "pb_energy": pb_energy, "tau_points": tau_points, "tau_weights": tau_weights, "trial": trial}


def mixing_matrix(mix_weights, slice_of_block, nbands):
    per_slice = mix_weights.shape[1]
    state_slice = jnp.repeat(slice_of_block, mix_weights.shape[0] // slice_of_block.shape[0])
    band_slice = jnp.arange(nbands, dtype=jnp.int32) // per_slice
    picked = state_slice[:, None] == band_slice[None, :]
    spread_weights = jnp.tile(mix_weights, (1, nbands // per_slice))
    return jnp.where(picked, spread_weights, jnp.zeros_like(spread_weights)).astype(jnp.bfloat16)


def contract(left, right):
    return lax.dot_general(left, right, (((1,), (1,)), ((), ())), preferred_element_type=jnp.float32)


def reference(occ_states, empty_states, mix_weights, slice_of_block, occ_energy, pb_energy, tau_points, tau_weights, trial):
    band_mix = mixing_matrix(mix_weights, slice_of_block, NPB)
    pseudo = jnp.dot(empty_states, band_mix, preferred_element_type=jnp.float32).astype(jnp.bfloat16)
    occ_wide = occ_states.astype(jnp.float32)
    pb_wide = pseudo.astype(jnp.float32)
    block_rows = math.gcd(NPTS, 1024)
    block_count = NPTS // block_rows
    row_occ = occ_states.reshape(block_count, block_rows, NOCC)
    row_pb = pseudo.reshape(block_count, block_rows, NPB)

    def one_block(row_pieces):
        rows_occ, rows_pb = row_pieces

        def one_time(summed, entries):
            time_point, weight = entries
            occ_scaled = (occ_wide * jnp.exp(occ_energy * time_point)[None, :]).astype(jnp.bfloat16)
            pb_scaled = (pb_wide * jnp.exp(-pb_energy * time_point)[None, :]).astype(jnp.bfloat16)
            g_occ = contract(rows_occ, occ_scaled)
            g_un = contract(rows_pb, pb_scaled)
            chi_tile = (weight * g_occ * g_un).astype(jnp.bfloat16)
            return summed + jnp.dot(chi_tile, trial, preferred_element_type=jnp.float32), None

        summed, _ = lax.scan(one_time, jnp.zeros((block_rows, NV), jnp.float32), (tau_points, tau_weights))
        return summed

    responses = lax.map(one_block, (row_occ, row_pb))
    return responses.reshape(NPTS, NV)
```

```python
import functools

import jax
import jax.numpy as jnp
from jax import lax
from jax.experimental import pallas as pl
from jax.experimental.pallas import tpu as pltpu
from jax.sharding import PartitionSpec as P

LANES = 128
VMEM = pl.BlockSpec(memory_space=pltpu.VMEM)
SMEM = pl.BlockSpec(memory_space=pltpu.SMEM)
PARAMS = pltpu.CompilerParams(vmem_limit_bytes=48 * 1024 * 1024)
NT = (((1,), (1,)), ((), ()))


def swap(block, axis, size, bit):
    return lax.ppermute(block, axis, [(i, i ^ bit) for i in range(size)])


def bits_of(size):
    return [1 << b for b in range(size.bit_length() - 1)]


def pack_kernel(slice_ref, tau_ref, weight_ref, mix_ref, empty_ref, occ_ref, trial_ref, packed_ref, times_ref, band_ref):
    nocc = occ_ref.shape[1]
    nbands, nempty = band_ref.shape
    per_slice = mix_ref.shape[0]
    width = nempty // slice_ref.shape[0]
    packed_ref[:, :nocc] = occ_ref[...]
    packed_ref[:, nocc + nbands :] = trial_ref[...]
    ntau = tau_ref.shape[0]
    for k in range(ntau):
        times_ref[k : k + 1, :] = jnp.full((1, LANES), tau_ref[k], jnp.float32)
        times_ref[ntau + k : ntau + k + 1, :] = jnp.full((1, LANES), weight_ref[k], jnp.float32)
    lane = lax.broadcasted_iota(jnp.int32, (per_slice, LANES), 1) // width
    per_chunk = LANES // width
    for chunk in range(nempty // LANES):
        at = slice(chunk * LANES, (chunk + 1) * LANES)
        state_slice = jnp.full((per_slice, LANES), slice_ref[chunk * per_chunk], jnp.int32)
        for b in range(1, per_chunk):
            state_slice = jnp.where(lane == b, slice_ref[chunk * per_chunk + b], state_slice)
        state_slice = state_slice.astype(jnp.float32).astype(jnp.bfloat16)
        mix = mix_ref[:, at].astype(jnp.bfloat16)
        for s in range(nbands // per_slice):
            band_ref[s * per_slice : (s + 1) * per_slice, at] = jnp.where(
                state_slice == jnp.bfloat16(s), mix, jnp.zeros_like(mix)
            )
    pseudo = lax.dot_general(empty_ref[...], band_ref[...], NT, preferred_element_type=jnp.float32)
    packed_ref[:, nocc : nocc + nbands] = pseudo.astype(jnp.bfloat16)


def respond(scaled_ref, weight_of, nocc, npb, cols_ref, ntau, rows):
    cols = cols_ref[...]
    g_occ = lax.dot_general(scaled_ref[:, :nocc], cols[:, :nocc], NT, preferred_element_type=jnp.float32)
    g_un = lax.dot_general(scaled_ref[:, nocc:], cols[:, nocc : nocc + npb], NT, preferred_element_type=jnp.float32)
    trial = cols[:, nocc + npb :]
    total = None
    for k in range(ntau):
        at = slice(k * rows, (k + 1) * rows)
        chi = (weight_of(k) * g_occ[at] * g_un[at]).astype(jnp.bfloat16)
        term = jnp.dot(chi, trial, preferred_element_type=jnp.float32)
        total = term if total is None else total + term
    return total


def first_kernel(nocc, npb, nplanes, ntau, *refs):
    own_ref, far_ref, times_ref, occ_energy_ref, pb_energy_ref = refs[:5]
    cols_refs = refs[5:-3]
    scaled_ref, weights_ref, total_ref = refs[-3:]
    rows = own_ref.shape[0]
    plane_rows = times_ref.shape[0] // nplanes
    for plane in range(nplanes):
        for k in range(ntau):
            point = times_ref[plane * plane_rows + k : plane * plane_rows + k + 1, 0:1]
            gain_occ = jnp.exp(occ_energy_ref[...] * point)
            gain_pb = jnp.exp(-pb_energy_ref[...] * point)
            at = plane * ntau + k
            weights_ref[at : at + 1, :] = times_ref[plane * plane_rows + ntau + k : plane * plane_rows + ntau + k + 1, :]
            for j, ref in enumerate((own_ref, far_ref)):
                to = slice((2 * at + j) * rows, (2 * at + j + 1) * rows)
                scaled_ref[to, :nocc] = (ref[:, :nocc].astype(jnp.float32) * gain_occ).astype(jnp.bfloat16)
                scaled_ref[to, nocc:] = (ref[:, nocc : nocc + npb].astype(jnp.float32) * gain_pb).astype(jnp.bfloat16)
    weight_of = lambda k: weights_ref[k : k + 1, 0:1]
    total = None
    for ref in cols_refs:
        term = respond(scaled_ref, weight_of, nocc, npb, ref, nplanes * ntau, 2 * rows)
        total = term if total is None else total + term
    total_ref[...] = total


def next_kernel(nocc, npb, ntau, scaled_ref, weights_ref, before_ref, cols_ref, total_ref):
    weight_of = lambda k: weights_ref[k : k + 1, 0:1]
    total_ref[...] = before_ref[...] + respond(
        scaled_ref, weight_of, nocc, npb, cols_ref, ntau, before_ref.shape[0]
    )


def local(sizes, occ_states, empty_states, mix_weights, slice_of_block, occ_energy, pb_energy, tau_points, tau_weights, trial):
    nrow, ncol, nplanes = sizes
    rows, nocc = occ_states.shape
    npb, nv = pb_energy.shape[0], trial.shape[1]
    ntau = tau_points.shape[0]
    plane_rows = -(-2 * ntau // 8) * 8
    width = nocc + npb + nv

    own, times = pl.pallas_call(
        pack_kernel,
        out_shape=(
            jax.ShapeDtypeStruct((rows, width), jnp.bfloat16),
            jax.ShapeDtypeStruct((plane_rows, LANES), jnp.float32),
        ),
        in_specs=[SMEM, SMEM, SMEM, VMEM, VMEM, VMEM, VMEM],
        out_specs=(VMEM, VMEM),
        scratch_shapes=[pltpu.VMEM((npb, empty_states.shape[1]), jnp.bfloat16)],
        compiler_params=PARAMS,
        name="pack",
    )(slice_of_block, tau_points, tau_weights, mix_weights.T, empty_states, occ_states, trial)

    col_bits, row_bits = bits_of(ncol), bits_of(nrow)
    near_bits, far_bit = col_bits[:-1], col_bits[-1]
    held = own
    for bit in near_bits:
        held = jnp.concatenate([held, swap(held, "col", ncol, bit)])
    far = swap(own, "col", ncol, far_bit)
    pieces = [held]
    for bit in row_bits[1:]:
        sent = pieces[0] if len(pieces) == 1 else jnp.concatenate(pieces)
        pieces.append(swap(sent, "row", nrow, bit))
    for bit in bits_of(nplanes):
        times = jnp.concatenate([times, swap(times, "tau", nplanes, bit)])
    paired = [swap(piece, "row", nrow, row_bits[0]) for piece in pieces]

    all_tau = nplanes * ntau
    scaled, weights, total = pl.pallas_call(
        functools.partial(first_kernel, nocc, npb, nplanes, ntau),
        out_shape=(
            jax.ShapeDtypeStruct((all_tau * 2 * rows, nocc + npb), jnp.bfloat16),
            jax.ShapeDtypeStruct((-(-all_tau // 8) * 8, LANES), jnp.float32),
            jax.ShapeDtypeStruct((2 * rows, nv), jnp.float32),
        ),
        in_specs=[VMEM] * 7,
        out_specs=(VMEM, VMEM, VMEM),
        compiler_params=PARAMS,
        name="first",
    )(own, far, times, occ_energy[None, :], pb_energy[None, :], pieces[0], paired[0])
    for piece in [p for pair in zip(pieces[1:], paired[1:]) for p in pair]:
        total = pl.pallas_call(
            functools.partial(next_kernel, nocc, npb, all_tau),
            out_shape=jax.ShapeDtypeStruct((2 * rows, nv), jnp.float32),
            in_specs=[VMEM] * 4,
            out_specs=VMEM,
            compiler_params=PARAMS,
            name="next",
        )(scaled, weights, total, piece)
    return total[:rows] + swap(total[rows:], "col", ncol, far_bit)


def solution(mesh):
    points = P(("col", "row"), None)
    in_specs = (points, points, P(), P(), P(), P(), P("tau"), P("tau"), points)
    sizes = tuple(mesh.shape[axis] for axis in ("row", "col", "tau"))
    return jax.shard_map(
        functools.partial(local, sizes), mesh=mesh, in_specs=in_specs, out_specs=points, check_vma=False
    )
```

```python
import functools

import jax
import jax.numpy as jnp
from jax import lax
from jax.experimental import pallas as pl
from jax.experimental.pallas import tpu as pltpu
from jax.sharding import PartitionSpec as P

LANES = 128
FIRST_COST = 10**9
VMEM = pl.BlockSpec(memory_space=pltpu.VMEM)
PARAMS = pltpu.CompilerParams(vmem_limit_bytes=48 * 1024 * 1024)
NT = (((1,), (1,)), ((), ()))


def plane_rows_of(ntau):
    return -(-2 * ntau // 8) * 8


def swap(block, axis, size, bit):
    return lax.ppermute(block, axis, [(i, i ^ bit) for i in range(size)])


def bits_of(size):
    return [1 << b for b in range(size.bit_length() - 1)]


def pack_kernel(
    slice_hbm, tau_hbm, weight_hbm, mix_hbm, empty_hbm, occ_hbm, trial_hbm,
    packed_ref, times_ref,
    partial_ref, slice_ref, tau_ref, weight_ref, mix_ref, empty_ref, sems,
):
    nocc = occ_hbm.shape[1]
    per_slice, nempty = mix_ref.shape
    nbands = partial_ref.shape[1]
    width = nempty // slice_ref.shape[0]
    per_chunk = LANES // width
    copies = [
        pltpu.make_async_copy(source, target, sems.at[i])
        for i, (source, target) in enumerate((
            (slice_hbm, slice_ref),
            (mix_hbm, mix_ref),
            (empty_hbm, empty_ref),
            (tau_hbm, tau_ref),
            (weight_hbm, weight_ref),
            (occ_hbm, packed_ref.at[:, :nocc]),
            (trial_hbm, packed_ref.at[:, nocc + nbands :]),
        ))
    ]
    for copy in copies:
        copy.start()
    partial_ref[...] = jnp.zeros_like(partial_ref)
    lane = lax.broadcasted_iota(jnp.int32, (per_slice, LANES), 1) // width
    inside = [lane == b for b in range(per_chunk)]
    for copy in copies[:3]:
        copy.wait()
    for chunk in range(nempty // LANES):
        at = slice(chunk * LANES, (chunk + 1) * LANES)
        mix = mix_ref[:, at]
        diagonal = jnp.concatenate(
            [jnp.where(inside[b], mix, jnp.zeros_like(mix)).astype(jnp.bfloat16) for b in range(per_chunk)], axis=0
        )
        share = lax.dot_general(diagonal, empty_ref[:, at], NT, preferred_element_type=jnp.float32)
        for b in range(per_chunk):
            first = pl.multiple_of(slice_ref[chunk * per_chunk + b] * per_slice, per_slice)
            to = pl.ds(first, per_slice)
            partial_ref[b, to, :] = partial_ref[b, to, :] + share[b * per_slice : (b + 1) * per_slice]
    pseudo = partial_ref[0]
    for b in range(1, per_chunk):
        pseudo = pseudo + partial_ref[b]
    packed_ref[:, nocc : nocc + nbands] = pseudo.T.astype(jnp.bfloat16)
    for copy in copies[3:]:
        copy.wait()
    ntau = tau_ref.shape[0]
    for k in range(ntau):
        times_ref[k : k + 1, :] = jnp.full((1, LANES), tau_ref[k], jnp.float32)
        times_ref[ntau + k : ntau + k + 1, :] = jnp.full((1, LANES), weight_ref[k], jnp.float32)


def scale(block_refs, times_ref, energy_refs, ntau, scaled_ref):
    rows = block_refs[0].shape[0]
    nocc = energy_refs[0].shape[1]
    at = 0
    for plane in range(0, times_ref.shape[0], plane_rows_of(ntau)):
        for k in range(plane, plane + ntau):
            point = times_ref[k : k + 1, 0:1]
            gain = jnp.concatenate(
                [jnp.exp(energy_refs[0][...] * point), jnp.exp(-energy_refs[1][...] * point)], axis=1
            )
            for ref in block_refs:
                states = ref[:, : scaled_ref.shape[1]].astype(jnp.float32)
                scaled_ref[at : at + rows, :] = (states * gain).astype(jnp.bfloat16)
                at += rows


def respond(scaled_ref, times_ref, nocc, ntau, cols_refs):
    nstates = scaled_ref.shape[1]
    planes = range(0, times_ref.shape[0], plane_rows_of(ntau))
    rows = scaled_ref.shape[0] // (len(planes) * ntau)
    total = None
    for cols_ref in cols_refs:
        cols = cols_ref[...]
        g_occ = lax.dot_general(scaled_ref[:, :nocc], cols[:, :nocc], NT, preferred_element_type=jnp.float32)
        g_un = lax.dot_general(scaled_ref[:, nocc:], cols[:, nocc:nstates], NT, preferred_element_type=jnp.float32)
        trial = cols[:, nstates:]
        at = 0
        for plane in planes:
            for k in range(plane + ntau, plane + 2 * ntau):
                weight = times_ref[k : k + 1, 0:1]
                chi = (weight * g_occ[at : at + rows] * g_un[at : at + rows]).astype(jnp.bfloat16)
                term = jnp.dot(chi, trial, preferred_element_type=jnp.float32)
                total = term if total is None else total + term
                at += rows
    return total


def first_kernel(ntau, own_ref, far_ref, times_ref, occ_energy_ref, pb_energy_ref, *refs):
    cols_refs, (scaled_ref, total_ref) = refs[:-2], refs[-2:]
    scale((own_ref, far_ref), times_ref, (occ_energy_ref, pb_energy_ref), ntau, scaled_ref)
    total_ref[...] = respond(scaled_ref, times_ref, occ_energy_ref.shape[1], ntau, cols_refs)


def second_kernel(
    ntau, nseen, own_ref, far_ref, times_ref, more_times_ref, occ_energy_ref, pb_energy_ref, scaled_ref, before_ref, *refs
):
    cols_refs, (more_scaled_ref, total_ref) = refs[:-2], refs[-2:]
    nocc = occ_energy_ref.shape[1]
    scale((own_ref, far_ref), more_times_ref, (occ_energy_ref, pb_energy_ref), ntau, more_scaled_ref)
    total = before_ref[...] + respond(more_scaled_ref, more_times_ref, nocc, ntau, cols_refs)
    if len(cols_refs) > nseen:
        total = total + respond(scaled_ref, times_ref, nocc, ntau, cols_refs[nseen:])
    total_ref[...] = total


def last_kernel(ntau, nocc, times_ref, more_times_ref, scaled_ref, more_scaled_ref, before_ref, cols_ref, total_ref):
    total_ref[...] = (
        before_ref[...]
        + respond(scaled_ref, times_ref, nocc, ntau, [cols_ref])
        + respond(more_scaled_ref, more_times_ref, nocc, ntau, [cols_ref])
    )


def call(kernel, outs, args, name, cost=None):
    return pl.pallas_call(
        kernel,
        out_shape=outs,
        in_specs=[VMEM] * len(args),
        out_specs=jax.tree.map(lambda _: VMEM, outs),
        compiler_params=PARAMS,
        cost_estimate=cost,
        name=name,
    )(*args)


def local(sizes, occ_states, empty_states, mix_weights, slice_of_block, occ_energy, pb_energy, tau_points, tau_weights, trial):
    nrow, ncol, nplanes = sizes
    rows, nocc = occ_states.shape
    npb, nv = pb_energy.shape[0], trial.shape[1]
    ntau = tau_points.shape[0]
    plane_rows = plane_rows_of(ntau)
    width = nocc + npb + nv

    nblocks, (nempty, per_slice) = slice_of_block.shape[0], mix_weights.shape
    operands = (slice_of_block, tau_points, tau_weights, mix_weights.T, empty_states, occ_states, trial)
    own, times = pl.pallas_call(
        pack_kernel,
        out_shape=(
            jax.ShapeDtypeStruct((rows, width), jnp.bfloat16),
            jax.ShapeDtypeStruct((plane_rows, LANES), jnp.float32),
        ),
        in_specs=[pl.BlockSpec(memory_space=pl.ANY)] * len(operands),
        out_specs=(VMEM, VMEM),
        scratch_shapes=[
            pltpu.VMEM((LANES * nblocks // nempty, npb, rows), jnp.float32),
            pltpu.SMEM((nblocks,), jnp.int32),
            pltpu.SMEM((ntau,), jnp.float32),
            pltpu.SMEM((ntau,), jnp.float32),
            pltpu.VMEM((per_slice, nempty), jnp.float32),
            pltpu.VMEM((rows, nempty), jnp.bfloat16),
            pltpu.SemaphoreType.DMA((len(operands),)),
        ],
        compiler_params=PARAMS,
        name="pack",
    )(*[pltpu.with_memory_space_constraint(operand, pltpu.HBM) for operand in operands])

    col_bits, row_bits = bits_of(ncol), bits_of(nrow)
    near_bits, far_bit = col_bits[:-1], col_bits[-1]
    received = []
    for bit in near_bits:
        received.append(swap(jnp.concatenate([own, *received]), "col", ncol, bit))
    near = jnp.concatenate([own, *received])
    far = swap(own, "col", ncol, far_bit)
    beside = swap(own, "row", nrow, row_bits[0])
    later = []
    for bit in row_bits[1:]:
        later.append(swap(jnp.concatenate([near, *later]), "row", nrow, bit))
    others = []
    for bit in bits_of(nplanes):
        others.append(swap(jnp.concatenate([times, *others]), "tau", nplanes, bit))
    more_times = jnp.concatenate(others)

    energies = (occ_energy[None, :], pb_energy[None, :])
    scaled_of = lambda times: jax.ShapeDtypeStruct(
        (times.shape[0] // plane_rows * ntau * 2 * rows, nocc + npb), jnp.bfloat16
    )
    total_of = jax.ShapeDtypeStruct((2 * rows, nv), jnp.float32)
    scaled, total = call(
        functools.partial(first_kernel, ntau),
        (scaled_of(times), total_of),
        (own, far, times, *energies, near, beside),
        "first",
        pl.CostEstimate(flops=FIRST_COST, bytes_accessed=10**6, transcendentals=0),
    )
    total, more_times, *later = lax.optimization_barrier((total, more_times, *later))
    last = swap(jnp.concatenate([*received, *later]), "row", nrow, row_bits[0])
    more_scaled, total = call(
        functools.partial(second_kernel, ntau, 2),
        (scaled_of(more_times), total_of),
        (own, far, times, more_times, *energies, scaled, total, near, beside, *later),
        "second",
    )
    total = call(
        functools.partial(last_kernel, ntau, nocc),
        total_of,
        (times, more_times, scaled, more_scaled, total, last),
        "last",
    )
    return total[:rows] + swap(total[rows:], "col", ncol, far_bit)


def solution(mesh):
    points = P(("col", "row"), None)
    in_specs = (points, points, P(), P(), P(), P(), P("tau"), P("tau"), points)
    sizes = tuple(mesh.shape[axis] for axis in ("row", "col", "tau"))
    return jax.shard_map(
        functools.partial(local, sizes), mesh=mesh, in_specs=in_specs, out_specs=points, check_vma=False
    )
```

```python
import functools

import jax
import jax.numpy as jnp
from jax import lax
from jax.experimental import pallas as pl
from jax.experimental.pallas import tpu as pltpu
from jax.sharding import PartitionSpec as P

LANES = 128
FIRST_COST = 10**9
VMEM = pl.BlockSpec(memory_space=pltpu.VMEM)
PARAMS = pltpu.CompilerParams(vmem_limit_bytes=48 * 1024 * 1024)
NT = (((1,), (1,)), ((), ()))


def plane_rows_of(ntau):
    return -(-2 * ntau // 8) * 8


def swap(block, axis, size, bit):
    return lax.ppermute(block, axis, [(i, i ^ bit) for i in range(size)])


def bits_of(size):
    return [1 << b for b in range(size.bit_length() - 1)]


def pack_kernel(
    slice_hbm, tau_hbm, weight_hbm, mix_hbm, empty_hbm, occ_hbm, trial_hbm,
    packed_ref, times_ref,
    partial_ref, slice_ref, tau_ref, weight_ref, mix_ref, empty_ref, sems,
):
    nocc = occ_hbm.shape[1]
    per_slice, nempty = mix_ref.shape
    nbands = partial_ref.shape[1]
    width = nempty // slice_ref.shape[0]
    per_chunk = LANES // width
    copies = [
        pltpu.make_async_copy(source, target, sems.at[i])
        for i, (source, target) in enumerate((
            (slice_hbm, slice_ref),
            (mix_hbm, mix_ref),
            (empty_hbm, empty_ref),
            (tau_hbm, tau_ref),
            (weight_hbm, weight_ref),
            (occ_hbm, packed_ref.at[:, :nocc]),
            (trial_hbm, packed_ref.at[:, nocc + nbands :]),
        ))
    ]
    for copy in copies:
        copy.start()
    partial_ref[...] = jnp.zeros_like(partial_ref)
    lane = lax.broadcasted_iota(jnp.int32, (per_slice, LANES), 1) // width
    inside = [lane == b for b in range(per_chunk)]
    for copy in copies[:3]:
        copy.wait()
    for chunk in range(nempty // LANES):
        at = slice(chunk * LANES, (chunk + 1) * LANES)
        mix = mix_ref[:, at]
        diagonal = jnp.concatenate(
            [jnp.where(inside[b], mix, jnp.zeros_like(mix)).astype(jnp.bfloat16) for b in range(per_chunk)], axis=0
        )
        share = lax.dot_general(diagonal, empty_ref[:, at], NT, preferred_element_type=jnp.float32)
        for b in range(per_chunk):
            first = pl.multiple_of(slice_ref[chunk * per_chunk + b] * per_slice, per_slice)
            to = pl.ds(first, per_slice)
            partial_ref[b, to, :] = partial_ref[b, to, :] + share[b * per_slice : (b + 1) * per_slice]
    pseudo = partial_ref[0]
    for b in range(1, per_chunk):
        pseudo = pseudo + partial_ref[b]
    packed_ref[:, nocc : nocc + nbands] = pseudo.T.astype(jnp.bfloat16)
    for copy in copies[3:]:
        copy.wait()
    ntau = tau_ref.shape[0]
    for k in range(ntau):
        times_ref[k : k + 1, :] = jnp.full((1, LANES), tau_ref[k], jnp.float32)
        times_ref[ntau + k : ntau + k + 1, :] = jnp.full((1, LANES), weight_ref[k], jnp.float32)


def scale(block_refs, times_ref, energy_refs, ntau, scaled_ref):
    rows = block_refs[0].shape[0]
    nocc = energy_refs[0].shape[1]
    at = 0
    for plane in range(0, times_ref.shape[0], plane_rows_of(ntau)):
        for k in range(plane, plane + ntau):
            point = times_ref[k : k + 1, 0:1]
            gain = jnp.concatenate(
                [jnp.exp(energy_refs[0][...] * point), jnp.exp(-energy_refs[1][...] * point)], axis=1
            )
            for ref in block_refs:
                states = ref[:, : scaled_ref.shape[1]].astype(jnp.float32)
                scaled_ref[at : at + rows, :] = (states * gain).astype(jnp.bfloat16)
                at += rows


def respond(scaled_ref, times_ref, nocc, ntau, cols_refs):
    nstates = scaled_ref.shape[1]
    planes = range(0, times_ref.shape[0], plane_rows_of(ntau))
    weights = [times_ref[plane + ntau + k : plane + ntau + k + 1, 0:1] for plane in planes for k in range(ntau)]
    rows = scaled_ref.shape[0] // len(weights)
    occ, pb, trial = (
        jnp.concatenate([ref[:, at] for ref in cols_refs], axis=0)
        for at in (slice(nocc), slice(nocc, nstates), slice(nstates, None))
    )
    g_occ = lax.dot_general(scaled_ref[:, :nocc], occ, NT, preferred_element_type=jnp.float32)
    g_un = lax.dot_general(scaled_ref[:, nocc:], pb, NT, preferred_element_type=jnp.float32)
    each = [slice(k * rows, (k + 1) * rows) for k in range(len(weights))]
    chi = jnp.concatenate([(w * g_occ[at] * g_un[at]).astype(jnp.bfloat16) for w, at in zip(weights, each)], axis=0)
    terms = jnp.dot(chi, trial, preferred_element_type=jnp.float32)
    return functools.reduce(jnp.add, [terms[at] for at in each])


def first_kernel(ntau, own_ref, far_ref, times_ref, occ_energy_ref, pb_energy_ref, *refs):
    cols_refs, (scaled_ref, total_ref) = refs[:-2], refs[-2:]
    scale((own_ref, far_ref), times_ref, (occ_energy_ref, pb_energy_ref), ntau, scaled_ref)
    total_ref[...] = respond(scaled_ref, times_ref, occ_energy_ref.shape[1], ntau, cols_refs)


def second_kernel(
    ntau, nseen, own_ref, far_ref, times_ref, more_times_ref, occ_energy_ref, pb_energy_ref, scaled_ref, before_ref, *refs
):
    cols_refs, (more_scaled_ref, total_ref) = refs[:-2], refs[-2:]
    nocc = occ_energy_ref.shape[1]
    scale((own_ref, far_ref), more_times_ref, (occ_energy_ref, pb_energy_ref), ntau, more_scaled_ref)
    total = before_ref[...] + respond(more_scaled_ref, more_times_ref, nocc, ntau, cols_refs)
    if len(cols_refs) > nseen:
        total = total + respond(scaled_ref, times_ref, nocc, ntau, cols_refs[nseen:])
    total_ref[...] = total


def last_kernel(ntau, nocc, times_ref, more_times_ref, scaled_ref, more_scaled_ref, before_ref, cols_ref, total_ref):
    total_ref[...] = (
        before_ref[...]
        + respond(scaled_ref, times_ref, nocc, ntau, [cols_ref])
        + respond(more_scaled_ref, more_times_ref, nocc, ntau, [cols_ref])
    )


def call(kernel, outs, args, name, cost=None):
    return pl.pallas_call(
        kernel,
        out_shape=outs,
        in_specs=[VMEM] * len(args),
        out_specs=jax.tree.map(lambda _: VMEM, outs),
        compiler_params=PARAMS,
        cost_estimate=cost,
        name=name,
    )(*args)


def local(sizes, occ_states, empty_states, mix_weights, slice_of_block, occ_energy, pb_energy, tau_points, tau_weights, trial):
    nrow, ncol, nplanes = sizes
    rows, nocc = occ_states.shape
    npb, nv = pb_energy.shape[0], trial.shape[1]
    ntau = tau_points.shape[0]
    plane_rows = plane_rows_of(ntau)
    width = nocc + npb + nv

    nblocks, (nempty, per_slice) = slice_of_block.shape[0], mix_weights.shape
    operands = (slice_of_block, tau_points, tau_weights, mix_weights.T, empty_states, occ_states, trial)
    own, times = pl.pallas_call(
        pack_kernel,
        out_shape=(
            jax.ShapeDtypeStruct((rows, width), jnp.bfloat16),
            jax.ShapeDtypeStruct((plane_rows, LANES), jnp.float32),
        ),
        in_specs=[pl.BlockSpec(memory_space=pl.ANY)] * len(operands),
        out_specs=(VMEM, VMEM),
        scratch_shapes=[
            pltpu.VMEM((LANES * nblocks // nempty, npb, rows), jnp.float32),
            pltpu.SMEM((nblocks,), jnp.int32),
            pltpu.SMEM((ntau,), jnp.float32),
            pltpu.SMEM((ntau,), jnp.float32),
            pltpu.VMEM((per_slice, nempty), jnp.float32),
            pltpu.VMEM((rows, nempty), jnp.bfloat16),
            pltpu.SemaphoreType.DMA((len(operands),)),
        ],
        compiler_params=PARAMS,
        name="pack",
    )(*[pltpu.with_memory_space_constraint(operand, pltpu.HBM) for operand in operands])

    col_bits, row_bits = bits_of(ncol), bits_of(nrow)
    near_bits, far_bit = col_bits[:-1], col_bits[-1]
    received = []
    for bit in near_bits:
        received.append(swap(jnp.concatenate([own, *received]), "col", ncol, bit))
    near = jnp.concatenate([own, *received])
    far = swap(own, "col", ncol, far_bit)
    beside = swap(near, "row", nrow, row_bits[0])
    later = []
    for bit in row_bits[1:]:
        later.append(swap(jnp.concatenate([near, *later]), "row", nrow, bit))
    others = []
    for bit in bits_of(nplanes):
        others.append(swap(jnp.concatenate([times, *others]), "tau", nplanes, bit))
    more_times = jnp.concatenate(others)

    energies = (occ_energy[None, :], pb_energy[None, :])
    scaled_of = lambda times: jax.ShapeDtypeStruct(
        (times.shape[0] // plane_rows * ntau * 2 * rows, nocc + npb), jnp.bfloat16
    )
    total_of = jax.ShapeDtypeStruct((2 * rows, nv), jnp.float32)
    scaled, total = call(
        functools.partial(first_kernel, ntau),
        (scaled_of(times), total_of),
        (own, far, times, *energies, near),
        "first",
        pl.CostEstimate(flops=FIRST_COST, bytes_accessed=10**6, transcendentals=0),
    )
    total, more_times, *later = lax.optimization_barrier((total, more_times, *later))
    last = swap(jnp.concatenate(later), "row", nrow, row_bits[0])
    more_scaled, total = call(
        functools.partial(second_kernel, ntau, 1),
        (scaled_of(more_times), total_of),
        (own, far, times, more_times, *energies, scaled, total, near, beside, *later),
        "second",
    )
    total = call(
        functools.partial(last_kernel, ntau, nocc),
        total_of,
        (times, more_times, scaled, more_scaled, total, last),
        "last",
    )
    return total[:rows] + swap(total[rows:], "col", ncol, far_bit)


def solution(mesh):
    points = P(("col", "row"), None)
    in_specs = (points, points, P(), P(), P(), P(), P("tau"), P("tau"), points)
    sizes = tuple(mesh.shape[axis] for axis in ("row", "col", "tau"))
    return jax.shard_map(
        functools.partial(local, sizes), mesh=mesh, in_specs=in_specs, out_specs=points, check_vma=False
    )
```

```python
import functools

import jax
import jax.numpy as jnp
from jax import lax
from jax.experimental import pallas as pl
from jax.experimental.pallas import tpu as pltpu
from jax.sharding import PartitionSpec as P

LANES = 128
KERNEL_COST = 10**9
SECOND_COST = 3 * 10**9
VMEM = pl.BlockSpec(memory_space=pltpu.VMEM)
PARAMS = pltpu.CompilerParams(vmem_limit_bytes=48 * 1024 * 1024)
NT = (((1,), (1,)), ((), ()))


def plane_rows_of(ntau):
    return -(-2 * ntau // 8) * 8


def swap(block, axis, size, bit):
    return lax.ppermute(block, axis, [(i, i ^ bit) for i in range(size)])


def bits_of(size):
    return [1 << b for b in range(size.bit_length() - 1)]


def pack_kernel(
    slice_hbm, tau_hbm, weight_hbm, mix_hbm, empty_hbm, occ_hbm, trial_hbm,
    packed_ref, times_ref,
    slice_ref, tau_ref, weight_ref, mix_ref, empty_ref, sems, *partial_refs,
):
    nocc = occ_hbm.shape[1]
    per_slice, nempty = mix_ref.shape
    nbands = partial_refs[0].shape[0]
    width = nempty // slice_ref.shape[0]
    per_chunk = LANES // width
    copies = [
        pltpu.make_async_copy(source, target, sems.at[i])
        for i, (source, target) in enumerate((
            (slice_hbm, slice_ref),
            (mix_hbm, mix_ref),
            (empty_hbm, empty_ref),
            (tau_hbm, tau_ref),
            (weight_hbm, weight_ref),
            (occ_hbm, packed_ref.at[:, :nocc]),
            (trial_hbm, packed_ref.at[:, nocc + nbands :]),
        ))
    ]
    for copy in copies:
        copy.start()
    for ref in partial_refs:
        ref[...] = jnp.zeros_like(ref)
    lane = lax.broadcasted_iota(jnp.int32, (per_slice, LANES), 1) // width
    inside = [lane == b for b in range(per_chunk)]
    for copy in copies[:3]:
        copy.wait()
    for chunk in range(nempty // LANES):
        at = slice(chunk * LANES, (chunk + 1) * LANES)
        mix = mix_ref[:, at]
        diagonal = jnp.concatenate(
            [jnp.where(inside[b], mix, jnp.zeros_like(mix)).astype(jnp.bfloat16) for b in range(per_chunk)], axis=0
        )
        share = lax.dot_general(diagonal, empty_ref[:, at], NT, preferred_element_type=jnp.float32)
        for b, ref in enumerate(partial_refs):
            first = pl.multiple_of(slice_ref[chunk * per_chunk + b] * per_slice, per_slice)
            to = pl.ds(first, per_slice)
            ref[to, :] = ref[to, :] + share[b * per_slice : (b + 1) * per_slice]
    pseudo = functools.reduce(jnp.add, [ref[...] for ref in partial_refs])
    packed_ref[:, nocc : nocc + nbands] = pseudo.T.astype(jnp.bfloat16)
    for copy in copies[3:]:
        copy.wait()
    ntau = tau_ref.shape[0]
    for k in range(ntau):
        times_ref[k : k + 1, :] = jnp.full((1, LANES), tau_ref[k], jnp.float32)
        times_ref[ntau + k : ntau + k + 1, :] = jnp.full((1, LANES), weight_ref[k], jnp.float32)


def times_in(times_refs, ntau):
    rows = [(ref, plane + k) for ref in times_refs for plane in range(0, ref.shape[0], plane_rows_of(ntau)) for k in range(ntau)]
    return [ref[k : k + 1, 0:1] for ref, k in rows], [ref[k + ntau : k + ntau + 1, 0:1] for ref, k in rows]


def scale(block_ref, points, energy_refs, scaled_ref, at=0):
    rows, nstates = block_ref.shape[0], scaled_ref.shape[1]
    states = block_ref[:, :nstates].astype(jnp.float32)
    for point in points:
        gain = jnp.concatenate([jnp.exp(energy_refs[0][...] * point), jnp.exp(-energy_refs[1][...] * point)], axis=1)
        scaled_ref[at : at + rows, :] = (states * gain).astype(jnp.bfloat16)
        at += rows


def respond(scaled_ref, weights, nocc, cols_refs):
    nstates = scaled_ref.shape[1]
    rows = scaled_ref.shape[0] // len(weights)
    occ, pb, trial = (
        jnp.concatenate([ref[:, at] for ref in cols_refs], axis=0)
        for at in (slice(nocc), slice(nocc, nstates), slice(nstates, None))
    )
    g_occ = lax.dot_general(scaled_ref[:, :nocc], occ, NT, preferred_element_type=jnp.float32)
    g_un = lax.dot_general(scaled_ref[:, nocc:], pb, NT, preferred_element_type=jnp.float32)
    each = [slice(k * rows, (k + 1) * rows) for k in range(len(weights))]
    chi = jnp.concatenate([(w * g_occ[at] * g_un[at]).astype(jnp.bfloat16) for w, at in zip(weights, each)], axis=0)
    terms = jnp.dot(chi, trial, preferred_element_type=jnp.float32)
    return functools.reduce(jnp.add, [terms[at] for at in each])


def first_kernel(
    ntau, cols_ref, own_ref, far_ref, times_ref, occ_energy_ref, pb_energy_ref, own_scaled_ref, scaled_ref, total_ref
):
    points, weights = times_in([times_ref], ntau)
    scale(far_ref, points, (occ_energy_ref, pb_energy_ref), scaled_ref)
    scale(own_ref, points, (occ_energy_ref, pb_energy_ref), own_scaled_ref)
    total_ref[...] = respond(scaled_ref, weights, occ_energy_ref.shape[1], [cols_ref])


def second_kernel(
    ntau, block_ref, times_ref, more_times_ref, occ_energy_ref, pb_energy_ref, seen_ref, before_ref, near_ref, *refs
):
    cols_refs, (scaled_ref, total_ref) = refs[:-2], refs[-2:]
    nocc, nseen = occ_energy_ref.shape[1], seen_ref.shape[0]
    more_points, more_weights = times_in([more_times_ref], ntau)
    weights = times_in([times_ref], ntau)[1] + more_weights
    scaled_ref[:nseen, :] = seen_ref[...]
    scale(block_ref, more_points, (occ_energy_ref, pb_energy_ref), scaled_ref, nseen)
    total_ref[...] = (
        before_ref[...]
        + respond(scaled_ref.at[nseen:], more_weights, nocc, [near_ref])
        + respond(scaled_ref, weights, nocc, cols_refs)
    )


def last_kernel(ntau, nocc, times_ref, more_times_ref, scaled_ref, before_ref, cols_ref, total_ref):
    weights = times_in([times_ref, more_times_ref], ntau)[1]
    total_ref[...] = before_ref[...] + respond(scaled_ref, weights, nocc, [cols_ref])


def whole_kernel(ntau, block_ref, times_ref, more_times_ref, occ_energy_ref, pb_energy_ref, seen_ref, *refs):
    cols_refs, (total_ref, scaled_ref) = refs[:-2], refs[-2:]
    nseen = seen_ref.shape[0]
    scaled_ref[:nseen, :] = seen_ref[...]
    scale(block_ref, times_in([more_times_ref], ntau)[0], (occ_energy_ref, pb_energy_ref), scaled_ref, nseen)
    weights = times_in([times_ref, more_times_ref], ntau)[1]
    total_ref[...] = respond(scaled_ref, weights, occ_energy_ref.shape[1], cols_refs)


def call(kernel, outs, args, name, cost, scratch=()):
    return pl.pallas_call(
        kernel,
        out_shape=outs,
        in_specs=[VMEM] * len(args),
        out_specs=jax.tree.map(lambda _: VMEM, outs),
        scratch_shapes=scratch,
        compiler_params=PARAMS,
        cost_estimate=pl.CostEstimate(flops=cost, bytes_accessed=10**6, transcendentals=0),
        name=name,
    )(*args)


def local(sizes, occ_states, empty_states, mix_weights, slice_of_block, occ_energy, pb_energy, tau_points, tau_weights, trial):
    nrow, ncol, nplanes = sizes
    rows, nocc = occ_states.shape
    npb, nv = pb_energy.shape[0], trial.shape[1]
    ntau = tau_points.shape[0]
    plane_rows = plane_rows_of(ntau)
    width = nocc + npb + nv

    nblocks, (nempty, per_slice) = slice_of_block.shape[0], mix_weights.shape
    operands = (slice_of_block, tau_points, tau_weights, mix_weights.T, empty_states, occ_states, trial)
    own, times = pl.pallas_call(
        pack_kernel,
        out_shape=(
            jax.ShapeDtypeStruct((rows, width), jnp.bfloat16),
            jax.ShapeDtypeStruct((plane_rows, LANES), jnp.float32),
        ),
        in_specs=[pl.BlockSpec(memory_space=pl.ANY)] * len(operands),
        out_specs=(VMEM, VMEM),
        scratch_shapes=[
            pltpu.SMEM((nblocks,), jnp.int32),
            pltpu.SMEM((ntau,), jnp.float32),
            pltpu.SMEM((ntau,), jnp.float32),
            pltpu.VMEM((per_slice, nempty), jnp.float32),
            pltpu.VMEM((rows, nempty), jnp.bfloat16),
            pltpu.SemaphoreType.DMA((len(operands),)),
            *[pltpu.VMEM((npb, rows), jnp.float32)] * (LANES * nblocks // nempty),
        ],
        compiler_params=PARAMS,
        name="pack",
    )(*[pltpu.with_memory_space_constraint(operand, pltpu.HBM) for operand in operands])

    col_bits, row_bits = bits_of(ncol), bits_of(nrow)
    near_bits, far_bit = col_bits[:-1], col_bits[-1]
    received = []
    for bit in near_bits:
        received.append(swap(jnp.concatenate([own, *received]), "col", ncol, bit))
    near = jnp.concatenate([own, *received])
    far = swap(own, "col", ncol, far_bit)
    beside = swap(near, "row", nrow, row_bits[0])
    later = []
    for bit in row_bits[1:]:
        later.append(swap(jnp.concatenate([near, *later]), "row", nrow, bit))
    others = []
    for bit in bits_of(nplanes):
        others.append(swap(jnp.concatenate([times, *others]), "tau", nplanes, bit))
    more_times = jnp.concatenate(others)

    energies = (occ_energy[None, :], pb_energy[None, :])
    scaled_of = lambda planes: jax.ShapeDtypeStruct((planes * ntau * rows, nocc + npb), jnp.bfloat16)
    total_of = jax.ShapeDtypeStruct((rows, nv), jnp.float32)
    own_scaled, scaled, far_total = call(
        functools.partial(first_kernel, ntau),
        (scaled_of(1), scaled_of(1), total_of),
        (near, own, far, times, *energies),
        "first",
        KERNEL_COST,
    )
    far_total, *later = lax.optimization_barrier((far_total, *later))
    last = swap(jnp.concatenate(later), "row", nrow, row_bits[0])
    scaled, far_total = call(
        functools.partial(second_kernel, ntau),
        (scaled_of(nplanes), total_of),
        (far, times, more_times, *energies, scaled, far_total, near, beside, *later),
        "second",
        SECOND_COST,
    )
    far_total = call(
        functools.partial(last_kernel, ntau, nocc),
        total_of,
        (times, more_times, scaled, far_total, last),
        "last",
        KERNEL_COST,
    )
    total = call(
        functools.partial(whole_kernel, ntau),
        total_of,
        (own, times, more_times, *energies, own_scaled, near, beside, *later, last),
        "whole",
        KERNEL_COST,
        [pltpu.VMEM(scaled_of(nplanes).shape, jnp.bfloat16)],
    )
    return total + swap(far_total, "col", ncol, far_bit)


def solution(mesh):
    points = P(("col", "row"), None)
    in_specs = (points, points, P(), P(), P(), P(), P("tau"), P("tau"), points)
    sizes = tuple(mesh.shape[axis] for axis in ("row", "col", "tau"))
    return jax.shard_map(
        functools.partial(local, sizes), mesh=mesh, in_specs=in_specs, out_specs=points, check_vma=False
    )
```

```python
import functools

import jax
import jax.numpy as jnp
from jax import lax
from jax.experimental import pallas as pl
from jax.experimental.pallas import tpu as pltpu
from jax.sharding import PartitionSpec as P

LANES = 128
KERNEL_COST = 10**9
SCALE_COST = 10**9
JOIN_COST = 10**9
VMEM = pl.BlockSpec(memory_space=pltpu.VMEM)
PARAMS = pltpu.CompilerParams(vmem_limit_bytes=48 * 1024 * 1024)
NT = (((1,), (1,)), ((), ()))


def plane_rows_of(ntau):
    return -(-2 * ntau // 8) * 8


def swap(block, axis, size, bit):
    return lax.ppermute(block, axis, [(i, i ^ bit) for i in range(size)])


def bits_of(size):
    return [1 << b for b in range(size.bit_length() - 1)]


def pack_kernel(
    slice_hbm, tau_hbm, weight_hbm, mix_hbm, empty_hbm, occ_hbm, trial_hbm, occ_energy_hbm, pb_energy_hbm,
    packed_ref, times_ref, code_ref, energy_ref,
    slice_ref, tau_ref, weight_ref, mix_ref, empty_ref, occ_energy_ref, pb_energy_ref, sems, *partial_refs,
):
    nocc = occ_hbm.shape[1]
    per_slice, nempty = mix_ref.shape
    nbands = partial_refs[0].shape[0]
    width = nempty // slice_ref.shape[0]
    per_chunk = LANES // width
    copies = [
        pltpu.make_async_copy(source, target, sems.at[i])
        for i, (source, target) in enumerate((
            (slice_hbm, slice_ref),
            (mix_hbm, mix_ref),
            (empty_hbm, empty_ref),
            (tau_hbm, tau_ref),
            (weight_hbm, weight_ref),
            (occ_hbm, packed_ref.at[:, :nocc]),
            (trial_hbm, packed_ref.at[:, nocc + nbands :]),
            (occ_energy_hbm, occ_energy_ref),
            (pb_energy_hbm, pb_energy_ref),
        ))
    ]
    for copy in copies:
        copy.start()
    for ref in partial_refs:
        ref[...] = jnp.zeros_like(ref)
    lane = lax.broadcasted_iota(jnp.int32, (per_slice, LANES), 1) // width
    inside = [lane == b for b in range(per_chunk)]
    for copy in copies[:3]:
        copy.wait()
    for chunk in range(nempty // LANES):
        at = slice(chunk * LANES, (chunk + 1) * LANES)
        mix = mix_ref[:, at]
        diagonal = jnp.concatenate(
            [jnp.where(inside[b], mix, jnp.zeros_like(mix)).astype(jnp.bfloat16) for b in range(per_chunk)], axis=0
        )
        share = lax.dot_general(diagonal, empty_ref[:, at], NT, preferred_element_type=jnp.float32)
        for b, ref in enumerate(partial_refs):
            first = pl.multiple_of(slice_ref[chunk * per_chunk + b] * per_slice, per_slice)
            to = pl.ds(first, per_slice)
            ref[to, :] = ref[to, :] + share[b * per_slice : (b + 1) * per_slice]
    pseudo = functools.reduce(jnp.add, [ref[...] for ref in partial_refs])
    packed_ref[:, nocc : nocc + nbands] = pseudo.T.astype(jnp.bfloat16)
    for copy in copies[3:]:
        copy.wait()
    energy_ref[:, :nocc] = occ_energy_ref[...][None, :]
    energy_ref[:, nocc:] = -pb_energy_ref[...][None, :]
    ntau = tau_ref.shape[0]
    code_ref[...] = jnp.zeros_like(code_ref)
    for k in range(ntau):
        for i, ref in enumerate((tau_ref, weight_ref)):
            rest = jnp.full((1, LANES), ref[k], jnp.float32)
            times_ref[i * ntau + k : i * ntau + k + 1, :] = rest
            for j in range(3):
                part = rest.astype(jnp.bfloat16)
                row = (3 * i + j) * ntau + k
                code_ref[row : row + 1, :] = part
                rest = rest - part.astype(jnp.float32)


def times_in(times_refs, ntau):
    rows = [(ref, plane + k) for ref in times_refs for plane in range(0, ref.shape[0], plane_rows_of(ntau)) for k in range(ntau)]
    return [ref[k : k + 1, 0:1] for ref, k in rows], [ref[k + ntau : k + ntau + 1, 0:1] for ref, k in rows]


def scale(block_ref, points, energy_ref, scaled_ref):
    rows, nstates = block_ref.shape[0], scaled_ref.shape[1]
    states = block_ref[:, :nstates].astype(jnp.float32)
    energy = energy_ref[...]
    for k, point in enumerate(points):
        scaled_ref[k * rows : (k + 1) * rows, :] = (states * jnp.exp(energy * point)).astype(jnp.bfloat16)


def respond(scaled_ref, weights, nocc, nv, cols_refs):
    nstates = scaled_ref.shape[1]
    rows = scaled_ref.shape[0] // len(weights)
    occ, pb, trial = (
        jnp.concatenate([ref[:, at] for ref in cols_refs], axis=0)
        for at in (slice(nocc), slice(nocc, nstates), slice(nstates, nstates + nv))
    )
    g_occ = lax.dot_general(scaled_ref[:, :nocc], occ, NT, preferred_element_type=jnp.float32)
    g_un = lax.dot_general(scaled_ref[:, nocc:], pb, NT, preferred_element_type=jnp.float32)
    each = [slice(k * rows, (k + 1) * rows) for k in range(len(weights))]
    chi = jnp.concatenate([(w * g_occ[at] * g_un[at]).astype(jnp.bfloat16) for w, at in zip(weights, each)], axis=0)
    terms = jnp.dot(chi, trial, preferred_element_type=jnp.float32)
    return functools.reduce(jnp.add, [terms[at] for at in each])


def join_kernel(*refs):
    *part_refs, joined_ref = refs
    at = 0
    for ref in part_refs:
        joined_ref[at : at + ref.shape[0], :] = ref[...]
        at += ref.shape[0]


def scale_kernel(ntau, block_ref, times_ref, energy_ref, scaled_ref):
    scale(block_ref, times_in([times_ref], ntau)[0], energy_ref, scaled_ref)


def far_kernel(ntau, nocc, nv, block_ref, times_ref, more_times_ref, energy_ref, seen_ref, *refs):
    cols_refs, (total_ref, scaled_ref) = refs[:-2], refs[-2:]
    nseen = seen_ref.shape[0]
    scaled_ref[:nseen, :] = seen_ref[...]
    scale(block_ref, times_in([more_times_ref], ntau)[0], energy_ref, scaled_ref.at[nseen:])
    total_ref[...] = respond(scaled_ref, times_in([times_ref, more_times_ref], ntau)[1], nocc, nv, cols_refs)


def own_kernel(ntau, nocc, nv, block_ref, times_ref, more_times_ref, energy_ref, *refs):
    cols_refs, (total_ref, scaled_ref) = refs[:-2], refs[-2:]
    points, weights = times_in([times_ref, more_times_ref], ntau)
    scale(block_ref, points, energy_ref, scaled_ref)
    total_ref[...] = respond(scaled_ref, weights, nocc, nv, cols_refs)


def call(kernel, outs, args, name, cost, scratch=()):
    return pl.pallas_call(
        kernel,
        out_shape=outs,
        in_specs=[VMEM] * len(args),
        out_specs=jax.tree.map(lambda _: VMEM, outs),
        scratch_shapes=scratch,
        compiler_params=PARAMS,
        cost_estimate=pl.CostEstimate(flops=cost, bytes_accessed=10**6, transcendentals=0),
        name=name,
    )(*args)


def local(sizes, occ_states, empty_states, mix_weights, slice_of_block, occ_energy, pb_energy, tau_points, tau_weights, trial):
    nrow, ncol, nplanes = sizes
    rows, nocc = occ_states.shape
    npb, nv = pb_energy.shape[0], trial.shape[1]
    ntau = tau_points.shape[0]
    plane_rows = plane_rows_of(ntau)
    width = nocc + npb + nv
    assert 6 * ntau <= rows

    nblocks, (nempty, per_slice) = slice_of_block.shape[0], mix_weights.shape
    operands = (slice_of_block, tau_points, tau_weights, mix_weights.T, empty_states, occ_states, trial)
    operands += (occ_energy, pb_energy)
    own, times, code, energy = pl.pallas_call(
        pack_kernel,
        out_shape=(
            jax.ShapeDtypeStruct((rows, width), jnp.bfloat16),
            jax.ShapeDtypeStruct((plane_rows, LANES), jnp.float32),
            jax.ShapeDtypeStruct((rows, LANES), jnp.bfloat16),
            jax.ShapeDtypeStruct((1, nocc + npb), jnp.float32),
        ),
        in_specs=[pl.BlockSpec(memory_space=pl.ANY)] * len(operands),
        out_specs=(VMEM,) * 4,
        scratch_shapes=[
            pltpu.SMEM((nblocks,), jnp.int32),
            pltpu.SMEM((ntau,), jnp.float32),
            pltpu.SMEM((ntau,), jnp.float32),
            pltpu.VMEM((per_slice, nempty), jnp.float32),
            pltpu.VMEM((rows, nempty), jnp.bfloat16),
            pltpu.VMEM((nocc,), jnp.float32),
            pltpu.VMEM((npb,), jnp.float32),
            pltpu.SemaphoreType.DMA((len(operands),)),
            *[pltpu.VMEM((npb, rows), jnp.float32)] * (LANES * nblocks // nempty),
        ],
        compiler_params=PARAMS,
        name="pack",
    )(*[pltpu.with_memory_space_constraint(operand, pltpu.HBM) for operand in operands])

    col_bits, row_bits = bits_of(ncol), bits_of(nrow)
    (core_bit, x_bit), col_bit, far_bit = row_bits[:2], col_bits[0], col_bits[-1]
    base = own
    for bit in col_bits[1:-1]:
        base = jnp.concatenate([base, swap(base, "col", ncol, bit)])
    for bit in row_bits[2:]:
        base = jnp.concatenate([base, swap(base, "row", nrow, bit)])
    nbase = base.shape[0]

    far = swap(own[:, : nocc + npb], "col", ncol, far_bit)
    beside = swap(base, "row", nrow, core_bit)
    index = lambda r, c, t: (r * ncol + c) * nplanes + t
    places = [(r, c, t) for r in range(nrow) for c in range(ncol) for t in range(nplanes)]
    across = lax.ppermute(
        base, ("row", "col", "tau"), [(index(r, c, t), index(r ^ x_bit, c ^ col_bit, t)) for r, c, t in places]
    )
    across_beside = swap(across, "row", nrow, core_bit)
    mixed = lax.ppermute(
        jnp.concatenate([jnp.concatenate([base, beside]), jnp.tile(code, (2 * base.shape[0] // rows, 1))], axis=1),
        ("row", "col", "tau"),
        [
            (index(r, c, t), index(r ^ x_bit, c, t ^ 1) if r & core_bit else index(r, c ^ col_bit, t))
            for r, c, t in places
        ],
    )
    early = (base, beside, across)
    joined = jax.ShapeDtypeStruct((sum(part.shape[0] for part in early), width), jnp.bfloat16)
    early = call(join_kernel, joined, early, "join", JOIN_COST)
    early, mixed = lax.optimization_barrier((early, mixed))
    far, across_beside = lax.optimization_barrier((far, across_beside))
    traded = swap(mixed, "row", nrow, core_bit)
    cols = (early, across_beside, mixed, traded)

    parts = jnp.where(
        lax.axis_index("row") & core_bit == 0, traded[: 6 * ntau, width:], mixed[: 6 * ntau, width:]
    ).astype(jnp.float32)
    parts = [parts[j * ntau : (j + 1) * ntau] for j in range(6)]
    padding = jnp.zeros((plane_rows - 2 * ntau, LANES), jnp.float32)
    more_times = jnp.concatenate([parts[0] + parts[1] + parts[2], parts[3] + parts[4] + parts[5], padding])
    for bit in bits_of(nplanes)[1:]:
        more_times = jnp.concatenate([more_times, swap(jnp.concatenate([times, more_times]), "tau", nplanes, bit)])

    scaled_of = lambda planes: jax.ShapeDtypeStruct((planes * ntau * rows, nocc + npb), jnp.bfloat16)
    total_of = jax.ShapeDtypeStruct((rows, nv), jnp.float32)
    scratch = [pltpu.VMEM(scaled_of(nplanes).shape, jnp.bfloat16)]
    scaled = call(functools.partial(scale_kernel, ntau), scaled_of(1), (far, times, energy), "scale", SCALE_COST)
    far_total = call(
        functools.partial(far_kernel, ntau, nocc, nv),
        total_of,
        (far, times, more_times, energy, scaled, *cols),
        "far",
        KERNEL_COST,
        scratch,
    )
    total = call(
        functools.partial(own_kernel, ntau, nocc, nv),
        total_of,
        (own, times, more_times, energy, *cols),
        "own",
        KERNEL_COST,
        scratch,
    )
    return swap(far_total, "col", ncol, far_bit) + total


def solution(mesh):
    points = P(("col", "row"), None)
    in_specs = (points, points, P(), P(), P(), P(), P("tau"), P("tau"), points)
    sizes = tuple(mesh.shape[axis] for axis in ("row", "col", "tau"))
    return jax.shard_map(
        functools.partial(local, sizes), mesh=mesh, in_specs=in_specs, out_specs=points, check_vma=False
    )
```

```python
import functools

import jax
import jax.numpy as jnp
from jax import lax
from jax.experimental import pallas as pl
from jax.experimental.pallas import tpu as pltpu
from jax.sharding import PartitionSpec as P

LANES = 128
KERNEL_COST = 10**9
SCALE_COST = 10**9
JOIN_COST = 10**9
VMEM = pl.BlockSpec(memory_space=pltpu.VMEM)
PARAMS = pltpu.CompilerParams(vmem_limit_bytes=48 * 1024 * 1024)
NT = (((1,), (1,)), ((), ()))


def plane_rows_of(ntau):
    return -(-2 * ntau // 8) * 8


def swap(block, axis, size, bit):
    return lax.ppermute(block, axis, [(i, i ^ bit) for i in range(size)])


def bits_of(size):
    return [1 << b for b in range(size.bit_length() - 1)]


def pack_kernel(
    slice_hbm, tau_hbm, weight_hbm, mix_hbm, empty_hbm, occ_hbm, trial_hbm, occ_energy_hbm, pb_energy_hbm,
    packed_ref, times_ref, code_ref, energy_ref,
    slice_ref, tau_ref, weight_ref, mix_ref, empty_ref, occ_energy_ref, pb_energy_ref, sems, *partial_refs,
):
    nocc = occ_hbm.shape[1]
    per_slice, nempty = mix_ref.shape
    nbands = partial_refs[0].shape[0]
    width = nempty // slice_ref.shape[0]
    per_chunk = LANES // width
    copies = [
        pltpu.make_async_copy(source, target, sems.at[i])
        for i, (source, target) in enumerate((
            (slice_hbm, slice_ref),
            (mix_hbm, mix_ref),
            (empty_hbm, empty_ref),
            (tau_hbm, tau_ref),
            (weight_hbm, weight_ref),
            (occ_hbm, packed_ref.at[:, :nocc]),
            (trial_hbm, packed_ref.at[:, nocc + nbands :]),
            (occ_energy_hbm, occ_energy_ref),
            (pb_energy_hbm, pb_energy_ref),
        ))
    ]
    for copy in copies:
        copy.start()
    for ref in partial_refs:
        ref[...] = jnp.zeros_like(ref)
    lane = lax.broadcasted_iota(jnp.int32, (per_slice, LANES), 1) // width
    inside = [lane == b for b in range(per_chunk)]
    for copy in copies[:3]:
        copy.wait()
    for chunk in range(nempty // LANES):
        at = slice(chunk * LANES, (chunk + 1) * LANES)
        mix = mix_ref[:, at]
        diagonal = jnp.concatenate(
            [jnp.where(inside[b], mix, jnp.zeros_like(mix)).astype(jnp.bfloat16) for b in range(per_chunk)], axis=0
        )
        share = lax.dot_general(diagonal, empty_ref[:, at], NT, preferred_element_type=jnp.float32)
        for b, ref in enumerate(partial_refs):
            first = pl.multiple_of(slice_ref[chunk * per_chunk + b] * per_slice, per_slice)
            to = pl.ds(first, per_slice)
            ref[to, :] = ref[to, :] + share[b * per_slice : (b + 1) * per_slice]
    pseudo = functools.reduce(jnp.add, [ref[...] for ref in partial_refs])
    packed_ref[:, nocc : nocc + nbands] = pseudo.T.astype(jnp.bfloat16)
    for copy in copies[3:]:
        copy.wait()
    energy_ref[:, :nocc] = occ_energy_ref[...][None, :]
    energy_ref[:, nocc:] = -pb_energy_ref[...][None, :]
    ntau = tau_ref.shape[0]
    row = lax.broadcasted_iota(jnp.int32, code_ref.shape, 0)
    code = jnp.zeros(code_ref.shape, jnp.float32)
    for k in range(ntau):
        for i, ref in enumerate((tau_ref, weight_ref)):
            rest = jnp.full((1, LANES), ref[k], jnp.float32)
            times_ref[i * ntau + k : i * ntau + k + 1, :] = rest
            for j in range(3):
                part = rest.astype(jnp.bfloat16).astype(jnp.float32)
                code = jnp.where(row == (3 * i + j) * ntau + k, part, code)
                rest = rest - part
    code_ref[...] = code.astype(jnp.bfloat16)


def times_in(times_refs, ntau):
    rows = [(ref, plane + k) for ref in times_refs for plane in range(0, ref.shape[0], plane_rows_of(ntau)) for k in range(ntau)]
    return [ref[k : k + 1, 0:1] for ref, k in rows], [ref[k + ntau : k + ntau + 1, 0:1] for ref, k in rows]


def scale(block_ref, points, energy_ref, scaled_ref):
    rows, nstates = block_ref.shape[0], scaled_ref.shape[1]
    states = block_ref[:, :nstates].astype(jnp.float32)
    energy = energy_ref[...]
    for k, point in enumerate(points):
        scaled_ref[k * rows : (k + 1) * rows, :] = (states * jnp.exp(energy * point)).astype(jnp.bfloat16)


def respond(scaled_ref, weights, nocc, nv, cols_refs):
    nstates = scaled_ref.shape[1]
    rows = scaled_ref.shape[0] // len(weights)
    occ, pb, trial = (
        jnp.concatenate([ref[:, at] for ref in cols_refs], axis=0)
        for at in (slice(nocc), slice(nocc, nstates), slice(nstates, nstates + nv))
    )
    g_occ = lax.dot_general(scaled_ref[:, :nocc], occ, NT, preferred_element_type=jnp.float32)
    g_un = lax.dot_general(scaled_ref[:, nocc:], pb, NT, preferred_element_type=jnp.float32)
    each = [slice(k * rows, (k + 1) * rows) for k in range(len(weights))]
    chi = jnp.concatenate([(w * g_occ[at] * g_un[at]).astype(jnp.bfloat16) for w, at in zip(weights, each)], axis=1)
    return jnp.dot(chi, jnp.concatenate([trial] * len(weights), axis=0), preferred_element_type=jnp.float32)


def join_kernel(*refs):
    *part_refs, joined_ref = refs
    at = 0
    for ref in part_refs:
        joined_ref[at : at + ref.shape[0], :] = ref[...]
        at += ref.shape[0]


def scale_kernel(ntau, block_ref, times_ref, energy_ref, scaled_ref):
    scale(block_ref, times_in([times_ref], ntau)[0], energy_ref, scaled_ref)


def far_kernel(ntau, nocc, nv, block_ref, times_ref, more_times_ref, energy_ref, seen_ref, *refs):
    cols_refs, (total_ref, scaled_ref) = refs[:-2], refs[-2:]
    nseen = seen_ref.shape[0]
    scaled_ref[:nseen, :] = seen_ref[...]
    scale(block_ref, times_in([more_times_ref], ntau)[0], energy_ref, scaled_ref.at[nseen:])
    total_ref[...] = respond(scaled_ref, times_in([times_ref, more_times_ref], ntau)[1], nocc, nv, cols_refs)


def own_kernel(ntau, nocc, nv, block_ref, times_ref, more_times_ref, energy_ref, *refs):
    cols_refs, (total_ref, scaled_ref) = refs[:-2], refs[-2:]
    points, weights = times_in([times_ref, more_times_ref], ntau)
    scale(block_ref, points, energy_ref, scaled_ref)
    total_ref[...] = respond(scaled_ref, weights, nocc, nv, cols_refs)


def call(kernel, outs, args, name, cost, scratch=()):
    return pl.pallas_call(
        kernel,
        out_shape=outs,
        in_specs=[VMEM] * len(args),
        out_specs=jax.tree.map(lambda _: VMEM, outs),
        scratch_shapes=scratch,
        compiler_params=PARAMS,
        cost_estimate=pl.CostEstimate(flops=cost, bytes_accessed=10**6, transcendentals=0),
        name=name,
    )(*args)


def local(sizes, occ_states, empty_states, mix_weights, slice_of_block, occ_energy, pb_energy, tau_points, tau_weights, trial):
    nrow, ncol, nplanes = sizes
    rows, nocc = occ_states.shape
    npb, nv = pb_energy.shape[0], trial.shape[1]
    ntau = tau_points.shape[0]
    plane_rows = plane_rows_of(ntau)
    width = nocc + npb + nv
    assert 6 * ntau <= rows

    nblocks, (nempty, per_slice) = slice_of_block.shape[0], mix_weights.shape
    operands = (slice_of_block, tau_points, tau_weights, mix_weights.T, empty_states, occ_states, trial)
    operands += (occ_energy, pb_energy)
    own, times, code, energy = pl.pallas_call(
        pack_kernel,
        out_shape=(
            jax.ShapeDtypeStruct((rows, width), jnp.bfloat16),
            jax.ShapeDtypeStruct((plane_rows, LANES), jnp.float32),
            jax.ShapeDtypeStruct((rows, LANES), jnp.bfloat16),
            jax.ShapeDtypeStruct((1, nocc + npb), jnp.float32),
        ),
        in_specs=[pl.BlockSpec(memory_space=pl.ANY)] * len(operands),
        out_specs=(VMEM,) * 4,
        scratch_shapes=[
            pltpu.SMEM((nblocks,), jnp.int32),
            pltpu.SMEM((ntau,), jnp.float32),
            pltpu.SMEM((ntau,), jnp.float32),
            pltpu.VMEM((per_slice, nempty), jnp.float32),
            pltpu.VMEM((rows, nempty), jnp.bfloat16),
            pltpu.VMEM((nocc,), jnp.float32),
            pltpu.VMEM((npb,), jnp.float32),
            pltpu.SemaphoreType.DMA((len(operands),)),
            *[pltpu.VMEM((npb, rows), jnp.float32)] * (LANES * nblocks // nempty),
        ],
        compiler_params=PARAMS,
        name="pack",
    )(*[pltpu.with_memory_space_constraint(operand, pltpu.HBM) for operand in operands])

    col_bits, row_bits = bits_of(ncol), bits_of(nrow)
    (core_bit, x_bit), col_bit, far_bit = row_bits[:2], col_bits[0], col_bits[-1]
    base = own
    for bit in col_bits[1:-1]:
        base = jnp.concatenate([base, swap(base, "col", ncol, bit)])
    for bit in row_bits[2:]:
        base = jnp.concatenate([base, swap(base, "row", nrow, bit)])
    nbase = base.shape[0]

    far = swap(own[:, : nocc + npb], "col", ncol, far_bit)
    beside = swap(base, "row", nrow, core_bit)
    index = lambda r, c, t: (r * ncol + c) * nplanes + t
    places = [(r, c, t) for r in range(nrow) for c in range(ncol) for t in range(nplanes)]
    across = lax.ppermute(
        base, ("row", "col", "tau"), [(index(r, c, t), index(r ^ x_bit, c ^ col_bit, t)) for r, c, t in places]
    )
    across_beside = swap(across, "row", nrow, core_bit)
    mixed = lax.ppermute(
        jnp.concatenate([jnp.concatenate([base, beside]), jnp.tile(code, (2 * base.shape[0] // rows, 1))], axis=1),
        ("row", "col", "tau"),
        [
            (index(r, c, t), index(r ^ x_bit, c, t ^ 1) if r & core_bit else index(r, c ^ col_bit, t))
            for r, c, t in places
        ],
    )
    early = (base, beside, across)
    joined = jax.ShapeDtypeStruct((sum(part.shape[0] for part in early), width), jnp.bfloat16)
    early = call(join_kernel, joined, early, "join", JOIN_COST)
    early, mixed = lax.optimization_barrier((early, mixed))
    far, across_beside = lax.optimization_barrier((far, across_beside))
    traded = swap(mixed, "row", nrow, core_bit)
    cols = (early, across_beside, mixed, traded)

    parts = jnp.where(
        lax.axis_index("row") & core_bit == 0, traded[: 6 * ntau, width:], mixed[: 6 * ntau, width:]
    ).astype(jnp.float32)
    parts = [parts[j * ntau : (j + 1) * ntau] for j in range(6)]
    padding = jnp.zeros((plane_rows - 2 * ntau, LANES), jnp.float32)
    more_times = jnp.concatenate([parts[0] + parts[1] + parts[2], parts[3] + parts[4] + parts[5], padding])
    for bit in bits_of(nplanes)[1:]:
        more_times = jnp.concatenate([more_times, swap(jnp.concatenate([times, more_times]), "tau", nplanes, bit)])

    scaled_of = lambda planes: jax.ShapeDtypeStruct((planes * ntau * rows, nocc + npb), jnp.bfloat16)
    total_of = jax.ShapeDtypeStruct((rows, nv), jnp.float32)
    scratch = [pltpu.VMEM(scaled_of(nplanes).shape, jnp.bfloat16)]
    scaled = call(functools.partial(scale_kernel, ntau), scaled_of(1), (far, times, energy), "scale", SCALE_COST)
    far_total = call(
        functools.partial(far_kernel, ntau, nocc, nv),
        total_of,
        (far, times, more_times, energy, scaled, *cols),
        "far",
        KERNEL_COST,
        scratch,
    )
    total = call(
        functools.partial(own_kernel, ntau, nocc, nv),
        total_of,
        (own, times, more_times, energy, *cols),
        "own",
        KERNEL_COST,
        scratch,
    )
    return swap(far_total, "col", ncol, far_bit) + total


def solution(mesh):
    points = P(("col", "row"), None)
    in_specs = (points, points, P(), P(), P(), P(), P("tau"), P("tau"), points)
    sizes = tuple(mesh.shape[axis] for axis in ("row", "col", "tau"))
    return jax.shard_map(
        functools.partial(local, sizes), mesh=mesh, in_specs=in_specs, out_specs=points, check_vma=False
    )
```

```python
import functools

import jax
import jax.numpy as jnp
from jax import lax
from jax.experimental import pallas as pl
from jax.experimental.pallas import tpu as pltpu
from jax.sharding import PartitionSpec as P

LANES = 128
KERNEL_COST = 10**9
SCALE_COST = 2 * 10**9
JOIN_COST = 10**9
VMEM = pl.BlockSpec(memory_space=pltpu.VMEM)
PARAMS = pltpu.CompilerParams(vmem_limit_bytes=48 * 1024 * 1024)
NT = (((1,), (1,)), ((), ()))


def plane_rows_of(ntau):
    return -(-2 * ntau // 8) * 8


def swap(block, axis, size, bit):
    return lax.ppermute(block, axis, [(i, i ^ bit) for i in range(size)])


def bits_of(size):
    return [1 << b for b in range(size.bit_length() - 1)]


def pack_kernel(
    slice_hbm, tau_hbm, weight_hbm, mix_hbm, empty_hbm, occ_hbm, trial_hbm, occ_energy_hbm, pb_energy_hbm,
    packed_ref, times_ref, energy_ref,
    slice_ref, tau_ref, weight_ref, mix_ref, empty_ref, occ_energy_ref, pb_energy_ref, sems, *partial_refs,
):
    nocc = occ_hbm.shape[1]
    per_slice, nempty = mix_ref.shape
    nbands = partial_refs[0].shape[0]
    width = nempty // slice_ref.shape[0]
    per_chunk = LANES // width
    copies = [
        pltpu.make_async_copy(source, target, sems.at[i])
        for i, (source, target) in enumerate((
            (slice_hbm, slice_ref),
            (mix_hbm, mix_ref),
            (empty_hbm, empty_ref),
            (tau_hbm, tau_ref),
            (weight_hbm, weight_ref),
            (occ_hbm, packed_ref.at[:, :nocc]),
            (trial_hbm, packed_ref.at[:, nocc + nbands :]),
            (occ_energy_hbm, occ_energy_ref),
            (pb_energy_hbm, pb_energy_ref),
        ))
    ]
    for copy in copies:
        copy.start()
    for ref in partial_refs:
        ref[...] = jnp.zeros_like(ref)
    lane = lax.broadcasted_iota(jnp.int32, (per_slice, LANES), 1) // width
    inside = [lane == b for b in range(per_chunk)]
    for copy in copies[:3]:
        copy.wait()
    for chunk in range(nempty // LANES):
        at = slice(chunk * LANES, (chunk + 1) * LANES)
        mix = mix_ref[:, at]
        diagonal = jnp.concatenate(
            [jnp.where(inside[b], mix, jnp.zeros_like(mix)).astype(jnp.bfloat16) for b in range(per_chunk)], axis=0
        )
        share = lax.dot_general(diagonal, empty_ref[:, at], NT, preferred_element_type=jnp.float32)
        for b, ref in enumerate(partial_refs):
            first = pl.multiple_of(slice_ref[chunk * per_chunk + b] * per_slice, per_slice)
            to = pl.ds(first, per_slice)
            ref[to, :] = ref[to, :] + share[b * per_slice : (b + 1) * per_slice]
    pseudo = functools.reduce(jnp.add, [ref[...] for ref in partial_refs])
    packed_ref[:, nocc : nocc + nbands] = pseudo.T.astype(jnp.bfloat16)
    for copy in copies[3:]:
        copy.wait()
    energy_ref[:, :nocc] = occ_energy_ref[...][None, :]
    energy_ref[:, nocc:] = -pb_energy_ref[...][None, :]
    ntau = tau_ref.shape[0]
    for k in range(ntau):
        times_ref[k : k + 1, :] = jnp.full((1, LANES), tau_ref[k], jnp.float32)
        times_ref[ntau + k : ntau + k + 1, :] = jnp.full((1, LANES), weight_ref[k], jnp.float32)


def times_in(times_refs, ntau):
    rows = [(ref, plane + k) for ref in times_refs for plane in range(0, ref.shape[0], plane_rows_of(ntau)) for k in range(ntau)]
    return [ref[k : k + 1, 0:1] for ref, k in rows], [ref[k + ntau : k + ntau + 1, 0:1] for ref, k in rows]


def scale(block_ref, points, energy_ref, scaled_ref):
    rows, nstates = block_ref.shape[0], scaled_ref.shape[1]
    states = block_ref[:, :nstates].astype(jnp.float32)
    energy = energy_ref[...]
    for k, point in enumerate(points):
        scaled_ref[k * rows : (k + 1) * rows, :] = (states * jnp.exp(energy * point)).astype(jnp.bfloat16)


def respond(scaled_ref, weights, nocc, cols_refs):
    nstates = scaled_ref.shape[1]
    rows = scaled_ref.shape[0] // len(weights)
    occ, pb, trial = (
        jnp.concatenate([ref[:, at] for ref in cols_refs], axis=0)
        for at in (slice(nocc), slice(nocc, nstates), slice(nstates, None))
    )
    g_occ = lax.dot_general(scaled_ref[:, :nocc], occ, NT, preferred_element_type=jnp.float32)
    g_un = lax.dot_general(scaled_ref[:, nocc:], pb, NT, preferred_element_type=jnp.float32)
    each = [slice(k * rows, (k + 1) * rows) for k in range(len(weights))]
    chi = jnp.concatenate([(w * g_occ[at] * g_un[at]).astype(jnp.bfloat16) for w, at in zip(weights, each)], axis=1)
    return jnp.dot(chi, jnp.concatenate([trial] * len(weights), axis=0), preferred_element_type=jnp.float32)


def join_kernel(*refs):
    *part_refs, joined_ref = refs
    at = 0
    for ref in part_refs:
        joined_ref[at : at + ref.shape[0], :] = ref[...]
        at += ref.shape[0]


def scale_kernel(ntau, block_ref, times_ref, more_times_ref, energy_ref, scaled_ref):
    scale(block_ref, times_in([times_ref, more_times_ref], ntau)[0], energy_ref, scaled_ref)


def respond_kernel(ntau, nocc, times_ref, more_times_ref, scaled_ref, *refs):
    cols_refs, total_ref = refs[:-1], refs[-1]
    total_ref[...] = respond(scaled_ref, times_in([times_ref, more_times_ref], ntau)[1], nocc, cols_refs)


def whole_kernel(ntau, nocc, block_ref, times_ref, more_times_ref, energy_ref, *refs):
    cols_refs, (total_ref, scaled_ref) = refs[:-2], refs[-2:]
    points, weights = times_in([times_ref, more_times_ref], ntau)
    scale(block_ref, points, energy_ref, scaled_ref)
    total_ref[...] = respond(scaled_ref, weights, nocc, cols_refs)


def call(kernel, outs, args, name, cost, scratch=()):
    return pl.pallas_call(
        kernel,
        out_shape=outs,
        in_specs=[VMEM] * len(args),
        out_specs=jax.tree.map(lambda _: VMEM, outs),
        scratch_shapes=scratch,
        compiler_params=PARAMS,
        cost_estimate=pl.CostEstimate(flops=cost, bytes_accessed=10**6, transcendentals=0),
        name=name,
    )(*args)


def local(sizes, occ_states, empty_states, mix_weights, slice_of_block, occ_energy, pb_energy, tau_points, tau_weights, trial):
    nrow, ncol, nplanes = sizes
    rows, nocc = occ_states.shape
    npb, nv = pb_energy.shape[0], trial.shape[1]
    ntau = tau_points.shape[0]
    plane_rows = plane_rows_of(ntau)
    width = nocc + npb + nv

    nblocks, (nempty, per_slice) = slice_of_block.shape[0], mix_weights.shape
    operands = (slice_of_block, tau_points, tau_weights, mix_weights.T, empty_states, occ_states, trial)
    operands += (occ_energy, pb_energy)
    own, times, energy = pl.pallas_call(
        pack_kernel,
        out_shape=(
            jax.ShapeDtypeStruct((rows, width), jnp.bfloat16),
            jax.ShapeDtypeStruct((plane_rows, LANES), jnp.float32),
            jax.ShapeDtypeStruct((1, nocc + npb), jnp.float32),
        ),
        in_specs=[pl.BlockSpec(memory_space=pl.ANY)] * len(operands),
        out_specs=(VMEM,) * 3,
        scratch_shapes=[
            pltpu.SMEM((nblocks,), jnp.int32),
            pltpu.SMEM((ntau,), jnp.float32),
            pltpu.SMEM((ntau,), jnp.float32),
            pltpu.VMEM((per_slice, nempty), jnp.float32),
            pltpu.VMEM((rows, nempty), jnp.bfloat16),
            pltpu.VMEM((nocc,), jnp.float32),
            pltpu.VMEM((npb,), jnp.float32),
            pltpu.SemaphoreType.DMA((len(operands),)),
            *[pltpu.VMEM((npb, rows), jnp.float32)] * (LANES * nblocks // nempty),
        ],
        compiler_params=PARAMS,
        name="pack",
    )(*[pltpu.with_memory_space_constraint(operand, pltpu.HBM) for operand in operands])

    col_bits, row_bits = bits_of(ncol), bits_of(nrow)
    (core_bit, x_bit), col_bit, far_bit = row_bits[:2], col_bits[0], col_bits[-1]
    base = own
    for bit in col_bits[1:-1]:
        base = jnp.concatenate([base, swap(base, "col", ncol, bit)])
    for bit in row_bits[2:]:
        base = jnp.concatenate([base, swap(base, "row", nrow, bit)])
    nbase = base.shape[0]

    far = swap(own, "col", ncol, far_bit)
    beside = swap(base, "row", nrow, core_bit)
    index = lambda r, c: r * ncol + c
    places = [(r, c) for r in range(nrow) for c in range(ncol)]
    across = lax.ppermute(base, ("row", "col"), [(index(r, c), index(r ^ x_bit, c ^ col_bit)) for r, c in places])
    across_beside = swap(across, "row", nrow, core_bit)
    mixed = lax.ppermute(
        jnp.concatenate([base, beside]),
        ("row", "col"),
        [(index(r, c), index(r ^ x_bit, c) if (r // core_bit + 1) % 2 else index(r, c ^ col_bit)) for r, c in places],
    )
    others = []
    for bit in bits_of(nplanes):
        others.append(swap(jnp.concatenate([times, *others]), "tau", nplanes, bit))
    more_times = jnp.concatenate(others)

    scaled_of = jax.ShapeDtypeStruct((nplanes * ntau * rows, nocc + npb), jnp.bfloat16)
    total_of = jax.ShapeDtypeStruct((rows, nv), jnp.float32)
    early = (base, beside, across)
    joined = jax.ShapeDtypeStruct((sum(part.shape[0] for part in early), width), jnp.bfloat16)
    early = call(join_kernel, joined, early, "join", JOIN_COST)
    early, mixed = lax.optimization_barrier((early, mixed))
    cols = (early, across_beside, mixed, swap(mixed, "row", nrow, core_bit))
    scaled = call(
        functools.partial(scale_kernel, ntau), scaled_of, (far, times, more_times, energy), "scale", SCALE_COST
    )
    far_total = call(
        functools.partial(respond_kernel, ntau, nocc), total_of, (times, more_times, scaled, *cols), "far", KERNEL_COST
    )
    total = call(
        functools.partial(whole_kernel, ntau, nocc),
        total_of,
        (own, times, more_times, energy, *cols),
        "own",
        KERNEL_COST,
        [pltpu.VMEM(scaled_of.shape, jnp.bfloat16)],
    )
    return swap(far_total, "col", ncol, far_bit) + total


def solution(mesh):
    points = P(("col", "row"), None)
    in_specs = (points, points, P(), P(), P(), P(), P("tau"), P("tau"), points)
    sizes = tuple(mesh.shape[axis] for axis in ("row", "col", "tau"))
    return jax.shard_map(
        functools.partial(local, sizes), mesh=mesh, in_specs=in_specs, out_specs=points, check_vma=False
    )
```

```python
import functools

import jax
import jax.numpy as jnp
from jax import lax
from jax.experimental import pallas as pl
from jax.experimental.pallas import tpu as pltpu
from jax.sharding import PartitionSpec as P

LANES = 128
KERNEL_COST = 10**9
SCALE_COST = 2 * 10**9
JOIN_COST = 10**9
VMEM = pl.BlockSpec(memory_space=pltpu.VMEM)
PARAMS = pltpu.CompilerParams(vmem_limit_bytes=48 * 1024 * 1024)
NT = (((1,), (1,)), ((), ()))


def plane_rows_of(ntau):
    return -(-2 * ntau // 8) * 8


def swap(block, axis, size, bit):
    return lax.ppermute(block, axis, [(i, i ^ bit) for i in range(size)])


def bits_of(size):
    return [1 << b for b in range(size.bit_length() - 1)]


def pack_kernel(
    slice_hbm, tau_hbm, weight_hbm, mix_hbm, empty_hbm, occ_hbm, trial_hbm, occ_energy_hbm, pb_energy_hbm,
    packed_ref, times_ref, energy_ref,
    slice_ref, tau_ref, weight_ref, mix_ref, empty_ref, occ_energy_ref, pb_energy_ref, sems, *partial_refs,
):
    nocc = occ_hbm.shape[1]
    per_slice, nempty = mix_ref.shape
    nbands = partial_refs[0].shape[0]
    width = nempty // slice_ref.shape[0]
    per_chunk = LANES // width
    copies = [
        pltpu.make_async_copy(source, target, sems.at[i])
        for i, (source, target) in enumerate((
            (slice_hbm, slice_ref),
            (mix_hbm, mix_ref),
            (empty_hbm, empty_ref),
            (tau_hbm, tau_ref),
            (weight_hbm, weight_ref),
            (occ_hbm, packed_ref.at[:, :nocc]),
            (trial_hbm, packed_ref.at[:, nocc + nbands :]),
            (occ_energy_hbm, occ_energy_ref),
            (pb_energy_hbm, pb_energy_ref),
        ))
    ]
    for copy in copies:
        copy.start()
    for ref in partial_refs:
        ref[...] = jnp.zeros_like(ref)
    lane = lax.broadcasted_iota(jnp.int32, (per_slice, LANES), 1) // width
    inside = [lane == b for b in range(per_chunk)]
    for copy in copies[:3]:
        copy.wait()
    for chunk in range(nempty // LANES):
        at = slice(chunk * LANES, (chunk + 1) * LANES)
        mix = mix_ref[:, at]
        diagonal = jnp.concatenate(
            [jnp.where(inside[b], mix, jnp.zeros_like(mix)).astype(jnp.bfloat16) for b in range(per_chunk)], axis=0
        )
        share = lax.dot_general(diagonal, empty_ref[:, at], NT, preferred_element_type=jnp.float32)
        for b, ref in enumerate(partial_refs):
            first = pl.multiple_of(slice_ref[chunk * per_chunk + b] * per_slice, per_slice)
            to = pl.ds(first, per_slice)
            ref[to, :] = ref[to, :] + share[b * per_slice : (b + 1) * per_slice]
    pseudo = functools.reduce(jnp.add, [ref[...] for ref in partial_refs])
    packed_ref[:, nocc : nocc + nbands] = pseudo.T.astype(jnp.bfloat16)
    for copy in copies[3:]:
        copy.wait()
    energy_ref[:, :nocc] = occ_energy_ref[...][None, :]
    energy_ref[:, nocc:] = -pb_energy_ref[...][None, :]
    ntau = tau_ref.shape[0]
    for k in range(ntau):
        times_ref[k : k + 1, :] = jnp.full((1, LANES), tau_ref[k], jnp.float32)
        times_ref[ntau + k : ntau + k + 1, :] = jnp.full((1, LANES), weight_ref[k], jnp.float32)


def times_in(times_refs, ntau):
    rows = [(ref, plane + k) for ref in times_refs for plane in range(0, ref.shape[0], plane_rows_of(ntau)) for k in range(ntau)]
    return [ref[k : k + 1, 0:1] for ref, k in rows], [ref[k + ntau : k + ntau + 1, 0:1] for ref, k in rows]


def scale(block_ref, points, energy_ref, scaled_ref):
    rows, nstates = block_ref.shape[0], scaled_ref.shape[1]
    states = block_ref[:, :nstates].astype(jnp.float32)
    energy = energy_ref[...]
    for k, point in enumerate(points):
        scaled_ref[k * rows : (k + 1) * rows, :] = (states * jnp.exp(energy * point)).astype(jnp.bfloat16)


def respond(scaled_ref, weights, nocc, cols_refs):
    nstates = scaled_ref.shape[1]
    rows = scaled_ref.shape[0] // len(weights)
    occ, pb, trial = (
        jnp.concatenate([ref[:, at] for ref in cols_refs], axis=0)
        for at in (slice(nocc), slice(nocc, nstates), slice(nstates, None))
    )
    g_occ = lax.dot_general(scaled_ref[:, :nocc], occ, NT, preferred_element_type=jnp.float32)
    g_un = lax.dot_general(scaled_ref[:, nocc:], pb, NT, preferred_element_type=jnp.float32)
    each = [slice(k * rows, (k + 1) * rows) for k in range(len(weights))]
    chi = jnp.concatenate([(w * g_occ[at] * g_un[at]).astype(jnp.bfloat16) for w, at in zip(weights, each)], axis=1)
    return jnp.dot(chi, jnp.concatenate([trial] * len(weights), axis=0), preferred_element_type=jnp.float32)


def join_kernel(*refs):
    *part_refs, joined_ref = refs
    at = 0
    for ref in part_refs:
        joined_ref[at : at + ref.shape[0], :] = ref[...]
        at += ref.shape[0]


def scale_kernel(ntau, block_ref, times_ref, more_times_ref, energy_ref, scaled_ref):
    scale(block_ref, times_in([times_ref, more_times_ref], ntau)[0], energy_ref, scaled_ref)


def respond_kernel(ntau, nocc, times_ref, more_times_ref, scaled_ref, *refs):
    cols_refs, total_ref = refs[:-1], refs[-1]
    total_ref[...] = respond(scaled_ref, times_in([times_ref, more_times_ref], ntau)[1], nocc, cols_refs)


def whole_kernel(ntau, nocc, block_ref, times_ref, more_times_ref, energy_ref, *refs):
    cols_refs, (total_ref, scaled_ref) = refs[:-2], refs[-2:]
    points, weights = times_in([times_ref, more_times_ref], ntau)
    scale(block_ref, points, energy_ref, scaled_ref)
    total_ref[...] = respond(scaled_ref, weights, nocc, cols_refs)


def call(kernel, outs, args, name, cost, scratch=()):
    return pl.pallas_call(
        kernel,
        out_shape=outs,
        in_specs=[VMEM] * len(args),
        out_specs=jax.tree.map(lambda _: VMEM, outs),
        scratch_shapes=scratch,
        compiler_params=PARAMS,
        cost_estimate=pl.CostEstimate(flops=cost, bytes_accessed=10**6, transcendentals=0),
        name=name,
    )(*args)


def local(sizes, occ_states, empty_states, mix_weights, slice_of_block, occ_energy, pb_energy, tau_points, tau_weights, trial):
    nrow, ncol, nplanes = sizes
    rows, nocc = occ_states.shape
    npb, nv = pb_energy.shape[0], trial.shape[1]
    ntau = tau_points.shape[0]
    plane_rows = plane_rows_of(ntau)
    width = nocc + npb + nv

    nblocks, (nempty, per_slice) = slice_of_block.shape[0], mix_weights.shape
    operands = (slice_of_block, tau_points, tau_weights, mix_weights.T, empty_states, occ_states, trial)
    operands += (occ_energy, pb_energy)
    own, times, energy = pl.pallas_call(
        pack_kernel,
        out_shape=(
            jax.ShapeDtypeStruct((rows, width), jnp.bfloat16),
            jax.ShapeDtypeStruct((plane_rows, LANES), jnp.float32),
            jax.ShapeDtypeStruct((1, nocc + npb), jnp.float32),
        ),
        in_specs=[pl.BlockSpec(memory_space=pl.ANY)] * len(operands),
        out_specs=(VMEM,) * 3,
        scratch_shapes=[
            pltpu.SMEM((nblocks,), jnp.int32),
            pltpu.SMEM((ntau,), jnp.float32),
            pltpu.SMEM((ntau,), jnp.float32),
            pltpu.VMEM((per_slice, nempty), jnp.float32),
            pltpu.VMEM((rows, nempty), jnp.bfloat16),
            pltpu.VMEM((nocc,), jnp.float32),
            pltpu.VMEM((npb,), jnp.float32),
            pltpu.SemaphoreType.DMA((len(operands),)),
            *[pltpu.VMEM((npb, rows), jnp.float32)] * (LANES * nblocks // nempty),
        ],
        compiler_params=PARAMS,
        name="pack",
    )(*[pltpu.with_memory_space_constraint(operand, pltpu.HBM) for operand in operands])

    col_bits, row_bits = bits_of(ncol), bits_of(nrow)
    (core_bit, x_bit), col_bit, far_bit = row_bits[:2], col_bits[0], col_bits[-1]
    base = own
    for bit in col_bits[1:-1]:
        base = jnp.concatenate([base, swap(base, "col", ncol, bit)])
    for bit in row_bits[2:]:
        base = jnp.concatenate([base, swap(base, "row", nrow, bit)])
    nbase = base.shape[0]

    far = swap(own, "col", ncol, far_bit)
    beside = swap(base, "row", nrow, core_bit)
    index = lambda r, c: r * ncol + c
    places = [(r, c) for r in range(nrow) for c in range(ncol)]
    across = lax.ppermute(base, ("row", "col"), [(index(r, c), index(r ^ x_bit, c ^ col_bit)) for r, c in places])
    across_beside = swap(across, "row", nrow, core_bit)
    mixed = lax.ppermute(
        jnp.concatenate([base, beside]),
        ("row", "col"),
        [(index(r, c), index(r ^ x_bit, c) if (r // core_bit + c // far_bit + 1) % 2 else index(r, c ^ col_bit)) for r, c in places],
    )
    others = []
    for bit in bits_of(nplanes):
        others.append(swap(jnp.concatenate([times, *others]), "tau", nplanes, bit))
    more_times = jnp.concatenate(others)

    scaled_of = jax.ShapeDtypeStruct((nplanes * ntau * rows, nocc + npb), jnp.bfloat16)
    total_of = jax.ShapeDtypeStruct((rows, nv), jnp.float32)
    early = (base, beside, across)
    joined = jax.ShapeDtypeStruct((sum(part.shape[0] for part in early), width), jnp.bfloat16)
    early = call(join_kernel, joined, early, "join", JOIN_COST)
    early, mixed = lax.optimization_barrier((early, mixed))
    cols = (early, across_beside, mixed, swap(mixed, "row", nrow, core_bit))
    scaled = call(
        functools.partial(scale_kernel, ntau), scaled_of, (far, times, more_times, energy), "scale", SCALE_COST
    )
    far_total = call(
        functools.partial(respond_kernel, ntau, nocc), total_of, (times, more_times, scaled, *cols), "far", KERNEL_COST
    )
    total = call(
        functools.partial(whole_kernel, ntau, nocc),
        total_of,
        (own, times, more_times, energy, *cols),
        "own",
        KERNEL_COST,
        [pltpu.VMEM(scaled_of.shape, jnp.bfloat16)],
    )
    return swap(far_total, "col", ncol, far_bit) + total


def solution(mesh):
    points = P(("col", "row"), None)
    in_specs = (points, points, P(), P(), P(), P(), P("tau"), P("tau"), points)
    sizes = tuple(mesh.shape[axis] for axis in ("row", "col", "tau"))
    return jax.shard_map(
        functools.partial(local, sizes), mesh=mesh, in_specs=in_specs, out_specs=points, check_vma=False
    )
```

```python
import functools

import jax
import jax.numpy as jnp
from jax import lax
from jax.experimental import pallas as pl
from jax.experimental.pallas import tpu as pltpu
from jax.sharding import PartitionSpec as P

LANES = 128
KERNEL_COST = 10**9
SCALE_COST = 2 * 10**9
JOIN_COST = 10**9
VMEM = pl.BlockSpec(memory_space=pltpu.VMEM)
PARAMS = pltpu.CompilerParams(vmem_limit_bytes=48 * 1024 * 1024)
NT = (((1,), (1,)), ((), ()))


def plane_rows_of(ntau):
    return -(-2 * ntau // 8) * 8


def swap(block, axis, size, bit):
    return lax.ppermute(block, axis, [(i, i ^ bit) for i in range(size)])


def bits_of(size):
    return [1 << b for b in range(size.bit_length() - 1)]


def pack_kernel(
    slice_hbm, tau_hbm, weight_hbm, mix_hbm, empty_hbm, occ_hbm, trial_hbm, occ_energy_hbm, pb_energy_hbm,
    packed_ref, states_ref, times_ref, energy_ref,
    slice_ref, tau_ref, weight_ref, mix_ref, empty_ref, occ_energy_ref, pb_energy_ref, sems, *partial_refs,
):
    nocc = occ_hbm.shape[1]
    per_slice, nempty = mix_ref.shape
    nbands = partial_refs[0].shape[0]
    width = nempty // slice_ref.shape[0]
    per_chunk = LANES // width
    copies = [
        pltpu.make_async_copy(source, target, sems.at[i])
        for i, (source, target) in enumerate((
            (slice_hbm, slice_ref),
            (mix_hbm, mix_ref),
            (empty_hbm, empty_ref),
            (tau_hbm, tau_ref),
            (weight_hbm, weight_ref),
            (occ_hbm, packed_ref.at[:, :nocc]),
            (trial_hbm, packed_ref.at[:, nocc + nbands :]),
            (occ_energy_hbm, occ_energy_ref),
            (pb_energy_hbm, pb_energy_ref),
        ))
    ]
    for copy in copies:
        copy.start()
    for ref in partial_refs:
        ref[...] = jnp.zeros_like(ref)
    lane = lax.broadcasted_iota(jnp.int32, (per_slice, LANES), 1) // width
    inside = [lane == b for b in range(per_chunk)]
    for copy in copies[:3]:
        copy.wait()
    for chunk in range(nempty // LANES):
        at = slice(chunk * LANES, (chunk + 1) * LANES)
        mix = mix_ref[:, at]
        diagonal = jnp.concatenate(
            [jnp.where(inside[b], mix, jnp.zeros_like(mix)).astype(jnp.bfloat16) for b in range(per_chunk)], axis=0
        )
        share = lax.dot_general(diagonal, empty_ref[:, at], NT, preferred_element_type=jnp.float32)
        for b, ref in enumerate(partial_refs):
            first = pl.multiple_of(slice_ref[chunk * per_chunk + b] * per_slice, per_slice)
            to = pl.ds(first, per_slice)
            ref[to, :] = ref[to, :] + share[b * per_slice : (b + 1) * per_slice]
    pseudo = functools.reduce(jnp.add, [ref[...] for ref in partial_refs])
    packed_ref[:, nocc : nocc + nbands] = pseudo.T.astype(jnp.bfloat16)
    for copy in copies[3:]:
        copy.wait()
    states_ref[...] = packed_ref[:, : nocc + nbands]
    energy_ref[:, :nocc] = occ_energy_ref[...][None, :]
    energy_ref[:, nocc:] = -pb_energy_ref[...][None, :]
    ntau = tau_ref.shape[0]
    for k in range(ntau):
        times_ref[k : k + 1, :] = jnp.full((1, LANES), tau_ref[k], jnp.float32)
        times_ref[ntau + k : ntau + k + 1, :] = jnp.full((1, LANES), weight_ref[k], jnp.float32)


def times_in(times_refs, ntau):
    rows = [(ref, plane + k) for ref in times_refs for plane in range(0, ref.shape[0], plane_rows_of(ntau)) for k in range(ntau)]
    return [ref[k : k + 1, 0:1] for ref, k in rows], [ref[k + ntau : k + ntau + 1, 0:1] for ref, k in rows]


def scale(block_ref, points, energy_ref, scaled_ref):
    rows, nstates = block_ref.shape[0], scaled_ref.shape[1]
    states = block_ref[:, :nstates].astype(jnp.float32)
    energy = energy_ref[...]
    for k, point in enumerate(points):
        scaled_ref[k * rows : (k + 1) * rows, :] = (states * jnp.exp(energy * point)).astype(jnp.bfloat16)


def respond(scaled_ref, weights, nocc, cols_refs):
    nstates = scaled_ref.shape[1]
    rows = scaled_ref.shape[0] // len(weights)
    occ, pb, trial = (
        jnp.concatenate([ref[:, at] for ref in cols_refs], axis=0)
        for at in (slice(nocc), slice(nocc, nstates), slice(nstates, None))
    )
    g_occ = lax.dot_general(scaled_ref[:, :nocc], occ, NT, preferred_element_type=jnp.float32)
    g_un = lax.dot_general(scaled_ref[:, nocc:], pb, NT, preferred_element_type=jnp.float32)
    each = [slice(k * rows, (k + 1) * rows) for k in range(len(weights))]
    chi = jnp.concatenate([(w * g_occ[at] * g_un[at]).astype(jnp.bfloat16) for w, at in zip(weights, each)], axis=1)
    return jnp.dot(chi, jnp.concatenate([trial] * len(weights), axis=0), preferred_element_type=jnp.float32)


def join_kernel(*refs):
    *part_refs, joined_ref = refs
    at = 0
    for ref in part_refs:
        joined_ref[at : at + ref.shape[0], :] = ref[...]
        at += ref.shape[0]


def scale_kernel(ntau, block_ref, times_ref, more_times_ref, energy_ref, scaled_ref):
    scale(block_ref, times_in([times_ref, more_times_ref], ntau)[0], energy_ref, scaled_ref)


def respond_kernel(ntau, nocc, times_ref, more_times_ref, scaled_ref, *refs):
    cols_refs, total_ref = refs[:-1], refs[-1]
    total_ref[...] = respond(scaled_ref, times_in([times_ref, more_times_ref], ntau)[1], nocc, cols_refs)


def whole_kernel(ntau, nocc, block_ref, times_ref, more_times_ref, energy_ref, *refs):
    cols_refs, (total_ref, scaled_ref) = refs[:-2], refs[-2:]
    points, weights = times_in([times_ref, more_times_ref], ntau)
    scale(block_ref, points, energy_ref, scaled_ref)
    total_ref[...] = respond(scaled_ref, weights, nocc, cols_refs)


def call(kernel, outs, args, name, cost, scratch=()):
    return pl.pallas_call(
        kernel,
        out_shape=outs,
        in_specs=[VMEM] * len(args),
        out_specs=jax.tree.map(lambda _: VMEM, outs),
        scratch_shapes=scratch,
        compiler_params=PARAMS,
        cost_estimate=pl.CostEstimate(flops=cost, bytes_accessed=10**6, transcendentals=0),
        name=name,
    )(*args)


def local(sizes, occ_states, empty_states, mix_weights, slice_of_block, occ_energy, pb_energy, tau_points, tau_weights, trial):
    nrow, ncol, nplanes = sizes
    rows, nocc = occ_states.shape
    npb, nv = pb_energy.shape[0], trial.shape[1]
    ntau = tau_points.shape[0]
    plane_rows = plane_rows_of(ntau)
    width = nocc + npb + nv

    nblocks, (nempty, per_slice) = slice_of_block.shape[0], mix_weights.shape
    operands = (slice_of_block, tau_points, tau_weights, mix_weights.T, empty_states, occ_states, trial)
    operands += (occ_energy, pb_energy)
    own, states, times, energy = pl.pallas_call(
        pack_kernel,
        out_shape=(
            jax.ShapeDtypeStruct((rows, width), jnp.bfloat16),
            jax.ShapeDtypeStruct((rows, nocc + npb), jnp.bfloat16),
            jax.ShapeDtypeStruct((plane_rows, LANES), jnp.float32),
            jax.ShapeDtypeStruct((1, nocc + npb), jnp.float32),
        ),
        in_specs=[pl.BlockSpec(memory_space=pl.ANY)] * len(operands),
        out_specs=(VMEM,) * 4,
        scratch_shapes=[
            pltpu.SMEM((nblocks,), jnp.int32),
            pltpu.SMEM((ntau,), jnp.float32),
            pltpu.SMEM((ntau,), jnp.float32),
            pltpu.VMEM((per_slice, nempty), jnp.float32),
            pltpu.VMEM((rows, nempty), jnp.bfloat16),
            pltpu.VMEM((nocc,), jnp.float32),
            pltpu.VMEM((npb,), jnp.float32),
            pltpu.SemaphoreType.DMA((len(operands),)),
            *[pltpu.VMEM((npb, rows), jnp.float32)] * (LANES * nblocks // nempty),
        ],
        compiler_params=PARAMS,
        name="pack",
    )(*[pltpu.with_memory_space_constraint(operand, pltpu.HBM) for operand in operands])

    col_bits, row_bits = bits_of(ncol), bits_of(nrow)
    (core_bit, x_bit), col_bit, far_bit = row_bits[:2], col_bits[0], col_bits[-1]
    base = own
    for bit in col_bits[1:-1]:
        base = jnp.concatenate([base, swap(base, "col", ncol, bit)])
    for bit in row_bits[2:]:
        base = jnp.concatenate([base, swap(base, "row", nrow, bit)])
    nbase = base.shape[0]

    far = swap(states, "col", ncol, far_bit)
    beside = swap(base, "row", nrow, core_bit)
    index = lambda r, c: r * ncol + c
    places = [(r, c) for r in range(nrow) for c in range(ncol)]
    across = lax.ppermute(base, ("row", "col"), [(index(r, c), index(r ^ x_bit, c ^ col_bit)) for r, c in places])
    across_beside = swap(across, "row", nrow, core_bit)
    mixed = lax.ppermute(
        jnp.concatenate([base, beside]),
        ("row", "col"),
        [(index(r, c), index(r ^ x_bit, c) if (r // core_bit + c // far_bit + 1) % 2 else index(r, c ^ col_bit)) for r, c in places],
    )
    sent_times, across = lax.optimization_barrier((times, across))
    others = []
    for bit in bits_of(nplanes):
        others.append(swap(jnp.concatenate([sent_times, *others]), "tau", nplanes, bit))
    more_times = jnp.concatenate(others)

    scaled_of = jax.ShapeDtypeStruct((nplanes * ntau * rows, nocc + npb), jnp.bfloat16)
    total_of = jax.ShapeDtypeStruct((rows, nv), jnp.float32)
    early = (base, beside, across)
    joined = jax.ShapeDtypeStruct((sum(part.shape[0] for part in early), width), jnp.bfloat16)
    early = call(join_kernel, joined, early, "join", JOIN_COST)
    early, mixed = lax.optimization_barrier((early, mixed))
    cols = (early, across_beside, mixed, swap(mixed, "row", nrow, core_bit))
    scaled = call(
        functools.partial(scale_kernel, ntau), scaled_of, (far, times, more_times, energy), "scale", SCALE_COST
    )
    far_total = call(
        functools.partial(respond_kernel, ntau, nocc), total_of, (times, more_times, scaled, *cols), "far", KERNEL_COST
    )
    total = call(
        functools.partial(whole_kernel, ntau, nocc),
        total_of,
        (own, times, more_times, energy, *cols),
        "own",
        KERNEL_COST,
        [pltpu.VMEM(scaled_of.shape, jnp.bfloat16)],
    )
    return swap(far_total, "col", ncol, far_bit) + total


def solution(mesh):
    points = P(("col", "row"), None)
    in_specs = (points, points, P(), P(), P(), P(), P("tau"), P("tau"), points)
    sizes = tuple(mesh.shape[axis] for axis in ("row", "col", "tau"))
    return jax.shard_map(
        functools.partial(local, sizes), mesh=mesh, in_specs=in_specs, out_specs=points, check_vma=False
    )
```

```python
import functools

import jax
import jax.numpy as jnp
from jax import lax
from jax.experimental import pallas as pl
from jax.experimental.pallas import tpu as pltpu
from jax.sharding import PartitionSpec as P

LANES = 128
KERNEL_COST = 10**9
SCALE_COST = 2 * 10**9
JOIN_COST = 10**9
VMEM = pl.BlockSpec(memory_space=pltpu.VMEM)
PARAMS = pltpu.CompilerParams(vmem_limit_bytes=48 * 1024 * 1024)
NT = (((1,), (1,)), ((), ()))


def plane_rows_of(ntau):
    return -(-2 * ntau // 8) * 8


def swap(block, axis, size, bit):
    return lax.ppermute(block, axis, [(i, i ^ bit) for i in range(size)])


def bits_of(size):
    return [1 << b for b in range(size.bit_length() - 1)]


def pack_kernel(
    slice_hbm, tau_hbm, weight_hbm, mix_hbm, empty_hbm, occ_hbm, trial_hbm, occ_energy_hbm, pb_energy_hbm,
    packed_ref, times_ref, energy_ref,
    slice_ref, tau_ref, weight_ref, mix_ref, empty_ref, occ_energy_ref, pb_energy_ref, sems, *partial_refs,
):
    nocc = occ_hbm.shape[1]
    per_slice, nempty = mix_ref.shape
    nbands = partial_refs[0].shape[0]
    width = nempty // slice_ref.shape[0]
    per_chunk = LANES // width
    copies = [
        pltpu.make_async_copy(source, target, sems.at[i])
        for i, (source, target) in enumerate((
            (empty_hbm, empty_ref),
            (mix_hbm, mix_ref),
            (slice_hbm, slice_ref),
            (tau_hbm, tau_ref),
            (weight_hbm, weight_ref),
            (occ_hbm, packed_ref.at[:, :nocc]),
            (trial_hbm, packed_ref.at[:, nocc + nbands :]),
            (occ_energy_hbm, occ_energy_ref),
            (pb_energy_hbm, pb_energy_ref),
        ))
    ]
    for copy in copies:
        copy.start()
    for ref in partial_refs:
        ref[...] = jnp.zeros_like(ref)
    lane = lax.broadcasted_iota(jnp.int32, (per_slice, LANES), 1) // width
    inside = [lane == b for b in range(per_chunk)]
    for copy in copies[:3]:
        copy.wait()
    for chunk in range(nempty // LANES):
        at = slice(chunk * LANES, (chunk + 1) * LANES)
        mix = mix_ref[:, at]
        diagonal = jnp.concatenate(
            [jnp.where(inside[b], mix, jnp.zeros_like(mix)).astype(jnp.bfloat16) for b in range(per_chunk)], axis=0
        )
        share = lax.dot_general(diagonal, empty_ref[:, at], NT, preferred_element_type=jnp.float32)
        for b, ref in enumerate(partial_refs):
            first = pl.multiple_of(slice_ref[chunk * per_chunk + b] * per_slice, per_slice)
            to = pl.ds(first, per_slice)
            ref[to, :] = ref[to, :] + share[b * per_slice : (b + 1) * per_slice]
    pseudo = functools.reduce(jnp.add, [ref[...] for ref in partial_refs])
    packed_ref[:, nocc : nocc + nbands] = pseudo.T.astype(jnp.bfloat16)
    for copy in copies[3:]:
        copy.wait()
    energy_ref[:, :nocc] = occ_energy_ref[...][None, :]
    energy_ref[:, nocc:] = -pb_energy_ref[...][None, :]
    ntau = tau_ref.shape[0]
    for k in range(ntau):
        times_ref[k : k + 1, :] = jnp.full((1, LANES), tau_ref[k], jnp.float32)
        times_ref[ntau + k : ntau + k + 1, :] = jnp.full((1, LANES), weight_ref[k], jnp.float32)


def times_in(times_refs, ntau):
    rows = [(ref, plane + k) for ref in times_refs for plane in range(0, ref.shape[0], plane_rows_of(ntau)) for k in range(ntau)]
    return [ref[k : k + 1, 0:1] for ref, k in rows], [ref[k + ntau : k + ntau + 1, 0:1] for ref, k in rows]


def scale(block_ref, points, energy_ref, scaled_ref):
    rows, nstates = block_ref.shape[0], scaled_ref.shape[1]
    states = block_ref[:, :nstates].astype(jnp.float32)
    energy = energy_ref[...]
    for k, point in enumerate(points):
        scaled_ref[k * rows : (k + 1) * rows, :] = (states * jnp.exp(energy * point)).astype(jnp.bfloat16)


def respond(scaled_ref, weights, nocc, cols_refs):
    nstates = scaled_ref.shape[1]
    rows = scaled_ref.shape[0] // len(weights)
    occ, pb, trial = (
        jnp.concatenate([ref[:, at] for ref in cols_refs], axis=0)
        for at in (slice(nocc), slice(nocc, nstates), slice(nstates, None))
    )
    g_occ = lax.dot_general(scaled_ref[:, :nocc], occ, NT, preferred_element_type=jnp.float32)
    g_un = lax.dot_general(scaled_ref[:, nocc:], pb, NT, preferred_element_type=jnp.float32)
    each = [slice(k * rows, (k + 1) * rows) for k in range(len(weights))]
    chi = jnp.concatenate([(w * g_occ[at] * g_un[at]).astype(jnp.bfloat16) for w, at in zip(weights, each)], axis=1)
    return jnp.dot(chi, jnp.concatenate([trial] * len(weights), axis=0), preferred_element_type=jnp.float32)


def join_kernel(*refs):
    *part_refs, joined_ref = refs
    at = 0
    for ref in part_refs:
        joined_ref[at : at + ref.shape[0], :] = ref[...]
        at += ref.shape[0]


def scale_kernel(ntau, block_ref, times_ref, more_times_ref, energy_ref, scaled_ref):
    scale(block_ref, times_in([times_ref, more_times_ref], ntau)[0], energy_ref, scaled_ref)


def respond_kernel(ntau, nocc, times_ref, more_times_ref, scaled_ref, *refs):
    cols_refs, total_ref = refs[:-1], refs[-1]
    total_ref[...] = respond(scaled_ref, times_in([times_ref, more_times_ref], ntau)[1], nocc, cols_refs)


def whole_kernel(ntau, nocc, block_ref, times_ref, more_times_ref, energy_ref, *refs):
    cols_refs, (total_ref, scaled_ref) = refs[:-2], refs[-2:]
    points, weights = times_in([times_ref, more_times_ref], ntau)
    scale(block_ref, points, energy_ref, scaled_ref)
    total_ref[...] = respond(scaled_ref, weights, nocc, cols_refs)


def call(kernel, outs, args, name, cost, scratch=()):
    return pl.pallas_call(
        kernel,
        out_shape=outs,
        in_specs=[VMEM] * len(args),
        out_specs=jax.tree.map(lambda _: VMEM, outs),
        scratch_shapes=scratch,
        compiler_params=PARAMS,
        cost_estimate=pl.CostEstimate(flops=cost, bytes_accessed=10**6, transcendentals=0),
        name=name,
    )(*args)


def local(sizes, occ_states, empty_states, mix_weights, slice_of_block, occ_energy, pb_energy, tau_points, tau_weights, trial):
    nrow, ncol, nplanes = sizes
    rows, nocc = occ_states.shape
    npb, nv = pb_energy.shape[0], trial.shape[1]
    ntau = tau_points.shape[0]
    plane_rows = plane_rows_of(ntau)
    width = nocc + npb + nv

    nblocks, (nempty, per_slice) = slice_of_block.shape[0], mix_weights.shape
    operands = (slice_of_block, tau_points, tau_weights, mix_weights.T, empty_states, occ_states, trial)
    operands += (occ_energy, pb_energy)
    own, times, energy = pl.pallas_call(
        pack_kernel,
        out_shape=(
            jax.ShapeDtypeStruct((rows, width), jnp.bfloat16),
            jax.ShapeDtypeStruct((plane_rows, LANES), jnp.float32),
            jax.ShapeDtypeStruct((1, nocc + npb), jnp.float32),
        ),
        in_specs=[pl.BlockSpec(memory_space=pl.ANY)] * len(operands),
        out_specs=(VMEM,) * 3,
        scratch_shapes=[
            pltpu.SMEM((nblocks,), jnp.int32),
            pltpu.SMEM((ntau,), jnp.float32),
            pltpu.SMEM((ntau,), jnp.float32),
            pltpu.VMEM((per_slice, nempty), jnp.float32),
            pltpu.VMEM((rows, nempty), jnp.bfloat16),
            pltpu.VMEM((nocc,), jnp.float32),
            pltpu.VMEM((npb,), jnp.float32),
            pltpu.SemaphoreType.DMA((len(operands),)),
            *[pltpu.VMEM((npb, rows), jnp.float32)] * (LANES * nblocks // nempty),
        ],
        compiler_params=PARAMS,
        name="pack",
    )(*[pltpu.with_memory_space_constraint(operand, pltpu.HBM) for operand in operands])

    col_bits, row_bits = bits_of(ncol), bits_of(nrow)
    (core_bit, x_bit), col_bit, far_bit = row_bits[:2], col_bits[0], col_bits[-1]
    base = own
    for bit in col_bits[1:-1]:
        base = jnp.concatenate([base, swap(base, "col", ncol, bit)])
    for bit in row_bits[2:]:
        base = jnp.concatenate([base, swap(base, "row", nrow, bit)])
    nbase = base.shape[0]

    far = swap(own, "col", ncol, far_bit)
    beside = swap(base, "row", nrow, core_bit)
    index = lambda r, c: r * ncol + c
    places = [(r, c) for r in range(nrow) for c in range(ncol)]
    across = lax.ppermute(base, ("row", "col"), [(index(r, c), index(r ^ x_bit, c ^ col_bit)) for r, c in places])
    across_beside = swap(across, "row", nrow, core_bit)
    mixed = lax.ppermute(
        jnp.concatenate([base, beside]),
        ("row", "col"),
        [(index(r, c), index(r ^ x_bit, c) if (r // core_bit + 1) % 2 else index(r, c ^ col_bit)) for r, c in places],
    )
    others = []
    for bit in bits_of(nplanes):
        others.append(swap(jnp.concatenate([times, *others]), "tau", nplanes, bit))
    more_times = jnp.concatenate(others)

    scaled_of = jax.ShapeDtypeStruct((nplanes * ntau * rows, nocc + npb), jnp.bfloat16)
    total_of = jax.ShapeDtypeStruct((rows, nv), jnp.float32)
    early = (base, beside, across)
    joined = jax.ShapeDtypeStruct((sum(part.shape[0] for part in early), width), jnp.bfloat16)
    early = call(join_kernel, joined, early, "join", JOIN_COST)
    early, mixed = lax.optimization_barrier((early, mixed))
    cols = (early, across_beside, mixed, swap(mixed, "row", nrow, core_bit))
    scaled = call(
        functools.partial(scale_kernel, ntau), scaled_of, (far, times, more_times, energy), "scale", SCALE_COST
    )
    far_total = call(
        functools.partial(respond_kernel, ntau, nocc), total_of, (times, more_times, scaled, *cols), "far", KERNEL_COST
    )
    total = call(
        functools.partial(whole_kernel, ntau, nocc),
        total_of,
        (own, times, more_times, energy, *cols),
        "own",
        KERNEL_COST,
        [pltpu.VMEM(scaled_of.shape, jnp.bfloat16)],
    )
    return swap(far_total, "col", ncol, far_bit) + total


def solution(mesh):
    points = P(("col", "row"), None)
    in_specs = (points, points, P(), P(), P(), P(), P("tau"), P("tau"), points)
    sizes = tuple(mesh.shape[axis] for axis in ("row", "col", "tau"))
    return jax.shard_map(
        functools.partial(local, sizes), mesh=mesh, in_specs=in_specs, out_specs=points, check_vma=False
    )
```

```python
import functools

import jax
import jax.numpy as jnp
from jax import lax
from jax.experimental import pallas as pl
from jax.experimental.pallas import tpu as pltpu
from jax.sharding import PartitionSpec as P

LANES = 128
KERNEL_COST = 10**9
SCALE_COST = 2 * 10**9
JOIN_COST = 10**9
VMEM = pl.BlockSpec(memory_space=pltpu.VMEM)
PARAMS = pltpu.CompilerParams(vmem_limit_bytes=48 * 1024 * 1024)
NT = (((1,), (1,)), ((), ()))


def plane_rows_of(ntau):
    return -(-2 * ntau // 8) * 8


def swap(block, axis, size, bit):
    return lax.ppermute(block, axis, [(i, i ^ bit) for i in range(size)])


def bits_of(size):
    return [1 << b for b in range(size.bit_length() - 1)]


def pack_kernel(
    slice_hbm, tau_hbm, weight_hbm, mix_hbm, empty_hbm, occ_hbm, trial_hbm, occ_energy_hbm, pb_energy_hbm,
    packed_ref, times_ref, energy_ref,
    slice_ref, tau_ref, weight_ref, mix_ref, empty_ref, occ_energy_ref, pb_energy_ref, sems, *partial_refs,
):
    nocc = occ_hbm.shape[1]
    per_slice, nempty = mix_ref.shape
    nbands = partial_refs[0].shape[0]
    width = nempty // slice_ref.shape[0]
    per_chunk = LANES // width
    copies = [
        pltpu.make_async_copy(source, target, sems.at[i])
        for i, (source, target) in enumerate((
            (empty_hbm, empty_ref),
            (mix_hbm, mix_ref),
            (slice_hbm, slice_ref),
            (tau_hbm, tau_ref),
            (weight_hbm, weight_ref),
            (occ_hbm, packed_ref.at[:, :nocc]),
            (trial_hbm, packed_ref.at[:, nocc + nbands :]),
            (occ_energy_hbm, occ_energy_ref),
            (pb_energy_hbm, pb_energy_ref),
        ))
    ]
    for copy in copies:
        copy.start()
    for ref in partial_refs:
        ref[...] = jnp.zeros_like(ref)
    lane = lax.broadcasted_iota(jnp.int32, (per_slice, LANES), 1) // width
    inside = [lane == b for b in range(per_chunk)]
    for copy in copies[:3]:
        copy.wait()
    for chunk in range(nempty // LANES):
        at = slice(chunk * LANES, (chunk + 1) * LANES)
        mix = mix_ref[:, at]
        diagonal = jnp.concatenate(
            [jnp.where(inside[b], mix, jnp.zeros_like(mix)).astype(jnp.bfloat16) for b in range(per_chunk)], axis=0
        )
        share = lax.dot_general(diagonal, empty_ref[:, at], NT, preferred_element_type=jnp.float32)
        for b, ref in enumerate(partial_refs):
            first = pl.multiple_of(slice_ref[chunk * per_chunk + b] * per_slice, per_slice)
            to = pl.ds(first, per_slice)
            ref[to, :] = ref[to, :] + share[b * per_slice : (b + 1) * per_slice]
    pseudo = functools.reduce(jnp.add, [ref[...] for ref in partial_refs])
    packed_ref[:, nocc : nocc + nbands] = pseudo.T.astype(jnp.bfloat16)
    for copy in copies[3:]:
        copy.wait()
    energy_ref[:, :nocc] = occ_energy_ref[...][None, :]
    energy_ref[:, nocc:] = -pb_energy_ref[...][None, :]
    ntau = tau_ref.shape[0]
    for k in range(ntau):
        times_ref[k : k + 1, :] = jnp.full((1, LANES), tau_ref[k], jnp.float32)
        times_ref[ntau + k : ntau + k + 1, :] = jnp.full((1, LANES), weight_ref[k], jnp.float32)


def times_in(times_refs, ntau):
    rows = [(ref, plane + k) for ref in times_refs for plane in range(0, ref.shape[0], plane_rows_of(ntau)) for k in range(ntau)]
    return [ref[k : k + 1, 0:1] for ref, k in rows], [ref[k + ntau : k + ntau + 1, 0:1] for ref, k in rows]


def scale(block_ref, points, energy_ref, scaled_ref):
    rows, nstates = block_ref.shape[0], scaled_ref.shape[1]
    states = block_ref[:, :nstates].astype(jnp.float32)
    energy = energy_ref[...]
    for k, point in enumerate(points):
        scaled_ref[k * rows : (k + 1) * rows, :] = (states * jnp.exp(energy * point)).astype(jnp.bfloat16)


def respond(scaled_ref, weights, nocc, cols_refs):
    nstates = scaled_ref.shape[1]
    rows = scaled_ref.shape[0] // len(weights)
    occ, pb, trial = (
        jnp.concatenate([ref[:, at] for ref in cols_refs], axis=0)
        for at in (slice(nocc), slice(nocc, nstates), slice(nstates, None))
    )
    g_occ = lax.dot_general(scaled_ref[:, :nocc], occ, NT, preferred_element_type=jnp.float32)
    g_un = lax.dot_general(scaled_ref[:, nocc:], pb, NT, preferred_element_type=jnp.float32)
    each = [slice(k * rows, (k + 1) * rows) for k in range(len(weights))]
    chi = jnp.concatenate([(w * g_occ[at] * g_un[at]).astype(jnp.bfloat16) for w, at in zip(weights, each)], axis=1)
    return jnp.dot(chi, jnp.concatenate([trial] * len(weights), axis=0), preferred_element_type=jnp.float32)


def join_kernel(*refs):
    *part_refs, joined_ref = refs
    at = 0
    for ref in part_refs:
        joined_ref[at : at + ref.shape[0], :] = ref[...]
        at += ref.shape[0]


def scale_kernel(ntau, block_ref, times_ref, more_times_ref, energy_ref, scaled_ref):
    scale(block_ref, times_in([times_ref, more_times_ref], ntau)[0], energy_ref, scaled_ref)


def respond_kernel(ntau, nocc, times_ref, more_times_ref, scaled_ref, *refs):
    cols_refs, total_ref = refs[:-1], refs[-1]
    total_ref[...] = respond(scaled_ref, times_in([times_ref, more_times_ref], ntau)[1], nocc, cols_refs)


def whole_kernel(ntau, nocc, block_ref, times_ref, more_times_ref, energy_ref, *refs):
    cols_refs, (total_ref, scaled_ref) = refs[:-2], refs[-2:]
    points, weights = times_in([times_ref, more_times_ref], ntau)
    scale(block_ref, points, energy_ref, scaled_ref)
    total_ref[...] = respond(scaled_ref, weights, nocc, cols_refs)


def call(kernel, outs, args, name, cost, scratch=()):
    return pl.pallas_call(
        kernel,
        out_shape=outs,
        in_specs=[VMEM] * len(args),
        out_specs=jax.tree.map(lambda _: VMEM, outs),
        scratch_shapes=scratch,
        compiler_params=PARAMS,
        cost_estimate=pl.CostEstimate(flops=cost, bytes_accessed=10**6, transcendentals=0),
        name=name,
    )(*args)


def local(sizes, occ_states, empty_states, mix_weights, slice_of_block, occ_energy, pb_energy, tau_points, tau_weights, trial):
    nrow, ncol, nplanes = sizes
    rows, nocc = occ_states.shape
    npb, nv = pb_energy.shape[0], trial.shape[1]
    ntau = tau_points.shape[0]
    plane_rows = plane_rows_of(ntau)
    width = nocc + npb + nv

    nblocks, (nempty, per_slice) = slice_of_block.shape[0], mix_weights.shape
    operands = (slice_of_block, tau_points, tau_weights, mix_weights.T, empty_states, occ_states, trial)
    operands += (occ_energy, pb_energy)
    own, times, energy = pl.pallas_call(
        pack_kernel,
        out_shape=(
            jax.ShapeDtypeStruct((rows, width), jnp.bfloat16),
            jax.ShapeDtypeStruct((plane_rows, LANES), jnp.float32),
            jax.ShapeDtypeStruct((1, nocc + npb), jnp.float32),
        ),
        in_specs=[pl.BlockSpec(memory_space=pl.ANY)] * len(operands),
        out_specs=(VMEM,) * 3,
        scratch_shapes=[
            pltpu.SMEM((nblocks,), jnp.int32),
            pltpu.SMEM((ntau,), jnp.float32),
            pltpu.SMEM((ntau,), jnp.float32),
            pltpu.VMEM((per_slice, nempty), jnp.float32),
            pltpu.VMEM((rows, nempty), jnp.bfloat16),
            pltpu.VMEM((nocc,), jnp.float32),
            pltpu.VMEM((npb,), jnp.float32),
            pltpu.SemaphoreType.DMA((len(operands),)),
            *[pltpu.VMEM((npb, rows), jnp.float32)] * (LANES * nblocks // nempty),
        ],
        compiler_params=PARAMS,
        name="pack",
    )(*[pltpu.with_memory_space_constraint(operand, pltpu.HBM) for operand in operands])

    col_bits, row_bits = bits_of(ncol), bits_of(nrow)
    (core_bit, x_bit), col_bit, far_bit = row_bits[:2], col_bits[0], col_bits[-1]
    base = own
    for bit in col_bits[1:-1]:
        base = jnp.concatenate([base, swap(base, "col", ncol, bit)])
    for bit in row_bits[2:]:
        base = jnp.concatenate([base, swap(base, "row", nrow, bit)])
    nbase = base.shape[0]

    far = swap(own, "col", ncol, far_bit)
    beside = swap(base, "row", nrow, core_bit)
    index = lambda r, c: r * ncol + c
    places = [(r, c) for r in range(nrow) for c in range(ncol)]
    across = lax.ppermute(base, ("row", "col"), [(index(r, c), index(r ^ x_bit, c ^ col_bit)) for r, c in places])
    across_beside = swap(across, "row", nrow, core_bit)
    mixed = lax.ppermute(
        jnp.concatenate([base, beside]),
        ("row", "col"),
        [(index(r, c), index(r ^ x_bit, c) if (r // core_bit + c // far_bit + 1) % 2 else index(r, c ^ col_bit)) for r, c in places],
    )
    others = []
    for bit in bits_of(nplanes):
        others.append(swap(jnp.concatenate([times, *others]), "tau", nplanes, bit))
    more_times = jnp.concatenate(others)

    scaled_of = jax.ShapeDtypeStruct((nplanes * ntau * rows, nocc + npb), jnp.bfloat16)
    total_of = jax.ShapeDtypeStruct((rows, nv), jnp.float32)
    early = (base, beside, across)
    joined = jax.ShapeDtypeStruct((sum(part.shape[0] for part in early), width), jnp.bfloat16)
    early = call(join_kernel, joined, early, "join", JOIN_COST)
    early, mixed = lax.optimization_barrier((early, mixed))
    cols = (early, across_beside, mixed, swap(mixed, "row", nrow, core_bit))
    scaled = call(
        functools.partial(scale_kernel, ntau), scaled_of, (far, times, more_times, energy), "scale", SCALE_COST
    )
    far_total = call(
        functools.partial(respond_kernel, ntau, nocc), total_of, (times, more_times, scaled, *cols), "far", KERNEL_COST
    )
    total = call(
        functools.partial(whole_kernel, ntau, nocc),
        total_of,
        (own, times, more_times, energy, *cols),
        "own",
        KERNEL_COST,
        [pltpu.VMEM(scaled_of.shape, jnp.bfloat16)],
    )
    return swap(far_total, "col", ncol, far_bit) + total


def solution(mesh):
    points = P(("col", "row"), None)
    in_specs = (points, points, P(), P(), P(), P(), P("tau"), P("tau"), points)
    sizes = tuple(mesh.shape[axis] for axis in ("row", "col", "tau"))
    return jax.shard_map(
        functools.partial(local, sizes), mesh=mesh, in_specs=in_specs, out_specs=points, check_vma=False
    )
```
